256 devices in a mesh: dp: 16 (over y, x_lo, core), tensor: 16 (over x_hi, z).
Axes of the slice: x: 4 (x_hi: 2, x_lo: 2; x = x_hi * 2 + x_lo), y: 4, z: 8, core: 2. Of those that a mesh axis runs over, the one named last changes fastest.
Arguments:
- layer_input: bfloat16 [32, 256, 4608], P('dp', 'tensor'), may hold values from -6 to 6
- out_grad: bfloat16 [32, 256, 4608], P('dp', 'tensor'), may hold values from -24 to 24
- loss_weight: float32 [32], P('dp'), may hold values from 0.1 to 1
- queries: bfloat16 [32, 256, 4096], P('dp', None, 'tensor'), may hold values from -6 to 6
- keys: bfloat16 [32, 256, 2048], P('dp', None, 'tensor'), may hold values from -6 to 6
- value_weight: bfloat16 [4608, 2048], P(None, 'tensor'), may hold values from -0.09375 to 0.09375
- output_weight: bfloat16 [4096, 4608], P('tensor'), may hold values from -0.09375 to 0.09375
- lengths: int32 [32], P('dp'), may hold values from 192 to 256, as said below
Outputs:
- grad_output: float32 [4096, 4608], P('tensor', 'dp')
- grad_value: float32 [4608, 2048], P('dp', 'tensor')
- grad_input: bfloat16 [32, 256, 4608], P('dp', 'tensor')
The draws below stay inside these ranges and needn't reach their ends.
Inputs may be any that keep to these rules, and one draw needn't show every extreme that they name: lengths[b] real tokens stand at the front of example b; some example is full.
All inputs are finite; a program needn't handle non-finite values.
Results may differ from the reference program's by a relative error of at most 0.007.
Values may be sent and summed in bfloat16 or wider, within the bound.
A program may use at most 128 MiB of HBM per device.

```python
import math
import jax
import jax.numpy as jnp
from jax import lax

D = 4608
HQ = 32
KVH = 16
HD = 128
QPRE = 144
SOFTCAP = 50
EX_DEV = 2
SEQ = 256
EXAMPLES = 32


def draw_lengths(key, part):
    key = jax.random.fold_in(key, 7)
    drawn_key, full_key, short_key = jax.random.split(key, 3)
    shortest = SEQ - SEQ // 4
    drawn = jax.random.randint(drawn_key, (EXAMPLES,), shortest, SEQ + 1)
    full_index = jax.random.randint(full_key, (), 0, EXAMPLES)
    short_index = (full_index + 1 + jax.random.randint(short_key, (), 0, EXAMPLES - 1)) % EXAMPLES
    example_index = jnp.arange(EXAMPLES)
    drawn = jnp.where(example_index == short_index, shortest, drawn)
    drawn = jnp.where(example_index == full_index, SEQ, drawn)
    return drawn.astype(jnp.int32)


def draw_out_grad(key, part):
    key = jax.random.fold_in(key, 11)
    noise_key, pair_key = jax.random.split(key)
    groups = EXAMPLES // EX_DEV
    pairing = jax.random.permutation(pair_key, groups)
    owning = jnp.arange(EXAMPLES) // EX_DEV
    column_block = jnp.arange(D) // (D // groups)
    spiked = pairing[owning][:, None] == column_block[None, :]
    booster = jnp.where(spiked, 4.0, 1.0).astype(jnp.float32)[:, None, :]
    entries = jax.random.truncated_normal(noise_key, -6.0, 6.0, (EXAMPLES, SEQ, D), jnp.float32)
    return (entries * booster).astype(jnp.bfloat16)


def block_levels(key, shape, cuts, low, largest):
    level = 1.0
    for dim, blocks in cuts:
        steps = jax.random.uniform(jax.random.fold_in(jax.random.fold_in(key, 6), dim), (blocks,), jnp.float32, low / len(cuts), largest / len(cuts))
        level = level * jnp.repeat(jnp.exp(steps), shape[dim] // blocks).reshape((-1,) + (1,) * (len(shape) - 1 - dim))
    return level


def gaussian(key, shape, deviation, most, cuts=(), held_as=jnp.bfloat16):
    array = deviation * jax.random.normal(key, shape, jnp.float32)
    if cuts:
        array = array * block_levels(key, shape, cuts, -0.22, 0.18)
    return jnp.clip(array, -most, most).astype(held_as)


def setup_inputs(seed: int = 0) -> dict:
    seeds = jax.random.split(jax.random.key(seed), 9)
    return {
        "layer_input": gaussian(seeds[0], (EXAMPLES, SEQ, D), 1.0, 6.0, ((0, 16), (1, 16))),
        "out_grad": draw_out_grad(jax.random.fold_in(seeds[8], 71), 0),
        "loss_weight": jnp.clip(jnp.exp(math.log(1.0) - 2.3025851 * jax.random.uniform(seeds[2], (EXAMPLES,), jnp.float32) ** block_levels(seeds[2], (EXAMPLES,), ((0, 16),), -0.2, 0.2)), 0.1, 1.0),
        "queries": gaussian(seeds[3], (EXAMPLES, SEQ, HQ * HD), 1.0, 6.0, ((0, 16), (2, 16))),
        "keys": gaussian(seeds[4], (EXAMPLES, SEQ, KVH * HD), 1.0, 6.0, ((0, 16), (2, 16))),
        "value_weight": gaussian(seeds[5], (D, KVH * HD), D ** -0.5, 0.09375, ((1, 16),)),
        "output_weight": gaussian(seeds[6], (HQ * HD, D), (HQ * HD) ** -0.5, 0.09375, ((0, 16),)),
        "lengths": draw_lengths(jax.random.fold_in(seeds[8], 71), 0),
    }


def reference(layer_input, out_grad, loss_weight, queries, keys, value_weight, output_weight, lengths):
    group = HQ // KVH
    bound = jnp.sqrt(jnp.float32(D * (HQ + KVH) * HD))
    position = jnp.arange(SEQ, dtype=jnp.int32)

    def one_example(carry, items):
        acc_out, acc_value = carry
        x_ex, dy_ex, w_ex, q_ex, k_ex, length = items
        live = position < length
        allowed = (position[None, :] <= position[:, None]) & live[None, :]
        values = jnp.dot(x_ex, value_weight, preferred_element_type=jnp.float32).astype(jnp.bfloat16)
        q_heads = q_ex.reshape(SEQ, KVH, group, HD).astype(jnp.float32)
        k_heads = k_ex.reshape(SEQ, KVH, HD).astype(jnp.float32)
        v_heads = values.reshape(SEQ, KVH, HD).astype(jnp.float32)
        raw = jnp.einsum('qkgd,skd->kgqs', q_heads, k_heads) * QPRE ** (-0.5)
        capped = SOFTCAP * jnp.tanh(raw / SOFTCAP)
        expo = jnp.where(allowed[None, None], jnp.exp(capped), 0.0)
        probs = (expo / lax.optimization_barrier(jnp.sum(expo, axis=-1, keepdims=True))).astype(jnp.bfloat16)
        probs32 = probs.astype(jnp.float32)
        context = jnp.einsum('kgqs,skd->qkgd', probs32, v_heads).astype(jnp.bfloat16).reshape(SEQ, HQ * HD)
        grad_at_out = (dy_ex.astype(jnp.float32) * w_ex * live[:, None].astype(jnp.float32)).astype(jnp.bfloat16)
        per_out = jnp.dot(context.T, grad_at_out, preferred_element_type=jnp.float32)
        grad_context = jnp.dot(grad_at_out, output_weight.T, preferred_element_type=jnp.float32).astype(jnp.bfloat16)
        grad_ctx_heads = grad_context.reshape(SEQ, KVH, group, HD).astype(jnp.float32)
        grad_values = jnp.einsum('kgqs,qkgd->skd', probs32, grad_ctx_heads).astype(jnp.bfloat16).reshape(SEQ, KVH * HD)
        per_value = jnp.dot(x_ex.T, grad_values, preferred_element_type=jnp.float32)
        grad_in = jnp.dot(grad_values, value_weight.T, preferred_element_type=jnp.float32).astype(jnp.bfloat16)
        sq_norm = jnp.sum(per_out * per_out) + jnp.sum(per_value * per_value)
        factor = bound / jnp.maximum(jnp.sqrt(sq_norm), bound)
        return ((acc_out + factor * per_out, acc_value + factor * per_value), grad_in)
    init = (jnp.zeros((HQ * HD, D), jnp.float32), jnp.zeros((D, KVH * HD), jnp.float32))
    (grad_output, grad_value), grad_input = lax.scan(one_example, init, (layer_input, out_grad, loss_weight, queries, keys, lengths))
    return (grad_output, grad_value, grad_input)
```

```python
import jax
import jax.numpy as jnp
from jax import lax
from jax.experimental import pallas as pl
from jax.experimental.pallas import tpu as pltpu
from jax.sharding import PartitionSpec as P

D = 4608
HQ = 32
KVH = 16
HD = 128
QPRE = 144
SOFTCAP = 50
SEQ = 256
NZ = 8
TOK = 16
HALF = D // 2
MESH = pl.DeviceIdType.MESH
F32 = jnp.float32
BF16 = jnp.bfloat16


def mo(value, multiple):
    return pl.multiple_of(value, multiple)


def dot(a, b):
    return jnp.dot(a, b, preferred_element_type=F32)


def kernel(
    lw_ref, len_ref, x_ref, g_ref, q_ref, k_ref, wv_ref, wo_ref,
    outt_ref, val_ref, gi_ref,
    xall, gall, xt, gt, gsend, qall, kall, wv, wvt, wo, probs, vall, call, dct, dvt, dv,
    gram, nbuf, dxf, zs, zr, gis, gir, csend, crecv, ssum,
    a1r, a2s, a2r, ua, a4r, a5s, a5r, b1r, b2s, b2r, ub, b4r, b5s, b5r,
    lsem, xsem, agsem, wsem, nsem, zsem, csem, rsem,
):
    dp, tn = lax.axis_index("dp"), lax.axis_index("tensor")
    h, z = lax.div(tn, NZ), lax.rem(tn, NZ)
    y, l, c = lax.div(dp, 4), lax.rem(lax.div(dp, 2), 2), lax.rem(dp, 2)
    x = 2 * h + l
    oh = 1 - h

    def zdev(step):
        return (dp, h * NZ + lax.rem(z + step + NZ, NZ))

    def ydev(step):
        return (lax.rem(y + step + 4, 4) * 4 + l * 2 + c, tn)

    def xpos(step):
        return lax.rem(x + step + 4, 4)

    def xdev(step):
        there = xpos(step)
        return (y * 4 + lax.rem(there, 2) * 2 + c, lax.div(there, 2) * NZ + z)

    partner = (dp, oh * NZ + z)
    cross = (y * 4 + (1 - l) * 2 + c, oh * NZ + z)
    core = (dp + 1 - 2 * c, tn)

    def rows(hs, zz):
        return pl.ds(mo(hs * (NZ * TOK) + zz * TOK, TOK), TOK)

    def remote(src, dst, sem, index, device):
        return pltpu.make_async_remote_copy(
            src_ref=src, dst_ref=dst, send_sem=sem.at[0, index], recv_sem=sem.at[1, index],
            device_id=device, device_id_type=MESH,
        )

    sent = []

    def send(src, dst, sem, index, device):
        copy = remote(src, dst, sem, index, device)
        copy.start()
        sent.append(copy)

    def arrived(dst, sem, index, device):
        remote(dst, dst, sem, index, device).wait_recv()

    my_rows, other_rows = rows(h, z), rows(oh, z)
    local = [
        pltpu.make_async_copy(x_ref.at[h], xall.at[my_rows], lsem.at[0]),
        pltpu.make_async_copy(q_ref.at[h], qall.at[:, pl.ds(mo(h * 256, 256), 256)], lsem.at[1]),
        pltpu.make_async_copy(k_ref.at[h], kall.at[:, pl.ds(mo(h * 128, 128), 128)], lsem.at[2]),
        pltpu.make_async_copy(wv_ref, wv.at[:, pl.ds(mo(h * 128, 128), 128)], lsem.at[3]),
        pltpu.make_async_copy(wo_ref, wo.at[pl.ds(mo(h * 256, 256), 256)], lsem.at[4]),
    ]
    for copy in local:
        copy.start()

    barrier = pltpu.get_barrier_semaphore()
    peers = [zdev(k) for k in range(1, NZ)] + [ydev(1), ydev(-1), xdev(1), xdev(-1), partner, core]
    for peer in peers:
        pl.semaphore_signal(barrier, inc=1, device_id=peer, device_id_type=MESH)

    position = tn * TOK + lax.broadcasted_iota(jnp.int32, (TOK, 1), 0)

    def weighted(e):
        live = (position < len_ref[e]).astype(F32)
        return (g_ref[e].astype(F32) * lw_ref[e] * live).astype(BF16)

    gall[my_rows, :] = weighted(h)
    gsend[...] = weighted(oh)

    pl.semaphore_wait(barrier, len(peers))

    arrs = (xall, gall)

    def ag_ref(arr, part, way, k, received):
        hs = h if part == 0 else oh
        back = k if received else k - 1
        origin = lax.rem(z + (NZ - back if way == 0 else back), NZ)
        columns = slice(None)
        if k == 4:
            columns = pl.ds(0, HALF) if way == 0 else pl.ds(HALF, HALF)
        return arrs[arr].at[rows(hs, origin), columns]

    def ag_index(arr, part, way, k):
        return ((arr * 2 + part) * 2 + way) * 4 + k - 1

    def ag_send(arr, part, k):
        for way in range(2):
            ref = ag_ref(arr, part, way, k, False)
            send(ref, ref, agsem, ag_index(arr, part, way, k), zdev(1 - 2 * way))

    def ag_wait(arr, part, k):
        for way in range(2):
            arrived(ag_ref(arr, part, way, k, True), agsem, ag_index(arr, part, way, k), zdev(1 - 2 * way))

    def ag_next(arr, part, k):
        ag_wait(arr, part, k)
        ag_send(arr, part, k + 1)

    def ex_refs(k, mine):
        hs = h if mine else oh
        qcol, kcol = pl.ds(mo(hs * 256, 256), 256), pl.ds(mo(hs * 128, 128), 128)
        return (
            xall.at[rows(hs, z)], gall.at[rows(hs, z)], qall.at[:, qcol], kall.at[:, kcol],
            gir,
        )[k]

    def ex_send(k, src):
        send(src, ex_refs(k, True), xsem, k, partner)

    def ex_wait(k):
        arrived(ex_refs(k, False), xsem, k, partner)

    def w_ref(arr, hs, yy, cc, part=None):
        piece = yy * 2 + cc
        size = (D // 8, 32)[arr]
        start = piece * size
        if part is not None:
            size = size // 2
            start = start + part * size
        ds = pl.ds(mo(start, 16), size)
        if arr == 0:
            return wv.at[ds, pl.ds(mo(hs * 128, 128), 128)]
        return wo.at[pl.ds(mo(hs * 256 + start, 16), size)]

    def w_first(arr):
        piece = y * 2 + c
        size = (D // 8, 32)[arr]
        src = (wv_ref, wo_ref)[arr].at[pl.ds(mo(piece * size, 16), size)]
        send(src, w_ref(arr, h, y, c), wsem, arr * 9, cross)

    def w_core(arr, step):
        yy = lax.rem(y + step, 4)
        ref = w_ref(arr, oh, yy, c)
        send(ref, ref, wsem, arr * 9 + 5 + step, core)

    def w_second(arr):
        ref = w_ref(arr, oh, y, c)
        arrived(ref, wsem, arr * 9, cross)
        send(ref, ref, wsem, arr * 9 + 1, ydev(1))
        send(ref, ref, wsem, arr * 9 + 2, ydev(-1))
        w_core(arr, 0)

    def w_third(arr):
        low, high = lax.rem(y + 3, 4), lax.rem(y + 1, 4)
        arrived(w_ref(arr, oh, low, c), wsem, arr * 9 + 1, ydev(1))
        ref = w_ref(arr, oh, low, c, 0)
        send(ref, ref, wsem, arr * 9 + 3, ydev(1))
        arrived(w_ref(arr, oh, high, c), wsem, arr * 9 + 2, ydev(-1))
        ref = w_ref(arr, oh, high, c, 1)
        send(ref, ref, wsem, arr * 9 + 4, ydev(-1))
        w_core(arr, 3)
        w_core(arr, 1)

    def w_fourth(arr):
        far = lax.rem(y + 2, 4)
        arrived(w_ref(arr, oh, far, c, 0), wsem, arr * 9 + 3, ydev(1))
        arrived(w_ref(arr, oh, far, c, 1), wsem, arr * 9 + 4, ydev(-1))
        w_core(arr, 2)

    def w_last(arr):
        for step in range(4):
            arrived(w_ref(arr, oh, lax.rem(y + step, 4), 1 - c), wsem, arr * 9 + 5 + step, core)

    def softmax(hs):
        length = len_ref[h]
        qpos = lax.broadcasted_iota(jnp.int32, (SEQ, SEQ), 0)
        kpos = lax.broadcasted_iota(jnp.int32, (SEQ, SEQ), 1)
        allowed = (kpos <= qpos) & (kpos < length)
        keys = kall[:, pl.ds(mo(hs * 128, 128), 128)]
        for g in range(2):
            query = qall[:, pl.ds(mo(hs * 256 + g * 128, 128), 128)]
            raw = lax.dot_general(query, keys, (((1,), (1,)), ((), ())), preferred_element_type=F32)
            capped = SOFTCAP * jnp.tanh(raw * (QPRE ** -0.5 / SOFTCAP))
            expo = jnp.where(allowed, jnp.exp(capped), 0.0)
            total = jnp.sum(expo, axis=1, keepdims=True)
            probs[hs * 2 + g] = (expo / total).astype(BF16)

    def transpose_half(src, dst, part):
        hs = h if part == 0 else oh
        ds = pl.ds(mo(hs * 128, 128), 128)

        def step(i, carry):
            cols = pl.ds(mo(i * 128, 128), 128)
            dst[cols, ds] = src[ds, cols].T
            return carry

        lax.fori_loop(0, D // 128, step, 0)

    def values(part):
        hs = h if part == 0 else oh
        ds = pl.ds(mo(hs * 128, 128), 128)
        vall[ds, :] = dot(xall[ds, :], wv[...]).astype(BF16)

    def contexts():
        for head in range(4):
            kv = head // 2
            call[:, head * 128:(head + 1) * 128] = dot(
                probs[head], vall[:, kv * 128:(kv + 1) * 128]
            ).astype(BF16)

    def wv_turn():
        def step(i, carry):
            ds = pl.ds(mo(i * 128, 128), 128)
            wvt[:, ds] = wv[ds, :].T
            return carry

        lax.fori_loop(0, D // 128, step, 0)

    def grad_contexts(part):
        hs = h if part == 0 else oh
        ds = pl.ds(mo(hs * 128, 128), 128)
        for half in range(2):
            dct[half * 256:(half + 1) * 256, ds] = dot(
                wo[half * 256:(half + 1) * 256, :], gt[:, ds]
            ).astype(BF16)

    def grad_values():
        for kv in range(2):
            both = dot(dct[kv * 256:kv * 256 + 128, :], probs[2 * kv])
            both += dot(dct[kv * 256 + 128:kv * 256 + 256, :], probs[2 * kv + 1])
            dvt[kv * 128:(kv + 1) * 128, :] = both.astype(BF16)
        dv[...] = dvt[...].T

    def x_gram():
        gram[...] = dot(xall[...], xt[...])

    def norm_send():
        cgram = lax.dot_general(call[...], call[...], (((1,), (1,)), ((), ())), preferred_element_type=F32)
        total = cgram * dot(gall[...], gt[...]) + gram[...] * dot(dv[...], dvt[...])
        total = jnp.sum(jnp.sum(total, axis=0, keepdims=True), axis=1, keepdims=True)
        nbuf[z] = jnp.broadcast_to(total, (8, 128))
        for k in range(1, NZ):
            send(nbuf.at[z], nbuf.at[z], nsem, k - 1, zdev(k))

    def norm_wait():
        for k in range(1, NZ):
            arrived(nbuf.at[lax.rem(z + NZ - k, NZ)], nsem, k - 1, zdev(k))
        sq = jnp.sum(nbuf[...], axis=0)[0:1, 0:1]
        bound = jnp.sqrt(F32(D * (HQ + KVH) * HD))
        return bound / jnp.maximum(jnp.sqrt(sq), bound)

    def dx_partial(part):
        hs = h if part == 0 else oh
        ds = pl.ds(mo(hs * 128, 128), 128)

        def step(i, carry):
            cols = pl.ds(mo(i * 512, 512), 512)
            dxf[ds, cols] = dot(dv[ds, :], wvt[:, cols])
            return carry

        lax.fori_loop(0, D // 512, step, 0)

    def z_cols(way):
        return pl.ds(0, HALF) if way == 0 else pl.ds(HALF, HALF)

    def z_index(part, way, k):
        return (part * 2 + way) * 4 + k - 1

    def z_start(part, way, k):
        index = z_index(part, way, k)
        src, dst = zs.at[index], zr.at[index]
        if k == 1:
            src, dst = src.at[:, z_cols(way)], dst.at[:, z_cols(way)]
        send(src, dst, zsem, index, zdev(1 - 2 * way))

    def z_arrived(part, way, k):
        index = z_index(part, way, k)
        dst = zr.at[index]
        if k == 1:
            dst = dst.at[:, z_cols(way)]
        arrived(dst, zsem, index, zdev(1 - 2 * way))

    def z_step(part, k):
        hs = h if part == 0 else oh
        for way in range(2):
            hops = 5 - k
            target = rows(hs, lax.rem(z + (hops if way == 0 else NZ - hops), NZ))
            index = z_index(part, way, k)
            if k == 1:
                zs[index, :, z_cols(way)] = dxf[target, z_cols(way)].astype(BF16)
            else:
                z_arrived(part, way, k - 1)
                if k == 2:
                    mine, rest = z_cols(way), z_cols(1 - way)
                    zs[index, :, mine] = (dxf[target, mine] + zr[index - 1, :, mine].astype(F32)).astype(BF16)
                    zs[index, :, rest] = dxf[target, rest].astype(BF16)
                else:
                    zs[index] = (dxf[target, :] + zr[index - 1].astype(F32)).astype(BF16)
            z_start(part, way, k)

    def z_final(part):
        hs = h if part == 0 else oh
        for way in range(2):
            z_arrived(part, way, 4)
        total = dxf[rows(hs, z), :]
        for way in range(2):
            total += zr[z_index(part, way, 4)].astype(F32)
        return total.astype(BF16)

    def grad_block(index, factor):
        ds = pl.ds(mo(index * 288, 16), 288)
        out = dot(gt[ds, :], call[...]) * factor
        value = dot(xt[ds, :], dv[...]) * factor
        return ((0, out[:, :256]), (256, value[:, :128]), (384, out[:, 256:]), (640, value[:, 128:]))

    def core_copy(n):
        return remote(csend.at[n], crecv.at[n], csem, n, core)

    def core_send(n, factor):
        for start, piece in grad_block(2 * n + 1 - c, factor):
            csend[n, :, start:start + piece.shape[1]] = piece.astype(BF16)
        core_copy(n).start()

    def core_sum(n, factor):
        core_copy(n).wait()
        for start, piece in grad_block(2 * n + c, factor):
            cols = slice(start, start + piece.shape[1])
            ssum[n, :, cols] = (piece + crecv[n, :, cols].astype(F32)).astype(BF16)

    def add(*pieces):
        total = pieces[0].astype(F32)
        for piece in pieces[1:]:
            total += piece.astype(F32)
        return total

    LOW, HIGH = pl.ds(0, 144), pl.ds(144, 144)

    def yp(step):
        return lax.rem(y + step + 4, 4)

    def hcols(hh):
        return pl.ds(mo(hh * 384, 128), 384)

    def xhl(step):
        there = xpos(step)
        return lax.div(there, 2), lax.rem(there, 2)

    def a_one():
        far = yp(2)
        send(ssum.at[2 * far, LOW], a1r.at[0], rsem, 0, ydev(1))
        send(ssum.at[2 * far + 1, LOW], a1r.at[1], rsem, 1, ydev(-1))
        send(ssum.at[2 * yp(1) + 1, LOW], a2r.at[0, 1], rsem, 2, ydev(1))
        send(ssum.at[2 * yp(-1), LOW], a2r.at[1, 0], rsem, 3, ydev(-1))

    def a_two():
        for way in range(2):
            step = 1 - 2 * way
            arrived(a1r.at[way], rsem, way, ydev(step))
            a2s[way] = add(ssum[2 * yp(step) + way, LOW, :], a1r[way]).astype(BF16)
            send(a2s.at[way], a2r.at[way, way], rsem, 4 + way, ydev(step))

    def a_three():
        arrived(a2r.at[0, 1], rsem, 2, ydev(1))
        arrived(a2r.at[1, 0], rsem, 3, ydev(-1))
        for way in range(2):
            arrived(a2r.at[way, way], rsem, 4 + way, ydev(1 - 2 * way))
        for ll in range(2):
            ua[ll] = add(ssum[2 * y + ll, LOW, :], a2r[0, ll], a2r[1, ll]).astype(BF16)
        ph, pll = xhl(2)
        send(ua.at[pll, pl.ds(0, 80), hcols(ph)], a4r.at[pl.ds(0, 80)], rsem, 6, xdev(1))
        send(ua.at[pll, pl.ds(80, 64), hcols(ph)], a4r.at[pl.ds(80, 64)], rsem, 7, xdev(-1))

    def a_four():
        for way, (start, size) in enumerate(((0, 80), (80, 64))):
            step = 1 - 2 * way
            ds, other = pl.ds(start, size), (pl.ds(80, 64), pl.ds(0, 80))[way]
            ph, pll = xhl(step)
            arrived(a4r.at[ds], rsem, 6 + way, xdev(step))
            a5s[way, ds, :] = add(ua[pll, ds, hcols(ph)], a4r[ds, :]).astype(BF16)
            a5s[way, other, :] = ua[pll, other, hcols(ph)]
            send(a5s.at[way], a5r.at[way], rsem, 8 + way, xdev(step))

    def a_five():
        for way in range(2):
            arrived(a5r.at[way], rsem, 8 + way, xdev(1 - 2 * way))
        total = add(ua[l, :, hcols(h)], a5r[0], a5r[1])
        outt_ref[0:144, :] = total[:, :256]
        val_ref[0:144, :] = total[:, 256:]

    def s_high(yy, ll, hh):
        return ssum.at[2 * yy + ll, HIGH, hcols(hh)]

    def b_one():
        ph, pll = xhl(2)
        for yy in range(4):
            send(s_high(yy, pll, ph), b1r.at[yy], rsem, 10 + yy, xdev(1 if yy < 2 else -1))
        for yy in range(4):
            way = 1 if yy < 2 else 0
            ph, pll = xhl(1 - 2 * way)
            send(s_high(yy, pll, ph), b2r.at[way, yy], rsem, 14 + yy, xdev(1 - 2 * way))

    def b_two():
        for yy in range(4):
            way = 0 if yy < 2 else 1
            step = 1 - 2 * way
            ph, pll = xhl(step)
            arrived(b1r.at[yy], rsem, 10 + yy, xdev(step))
            b2s[yy] = add(ssum[2 * yy + pll, HIGH, hcols(ph)], b1r[yy]).astype(BF16)
            send(b2s.at[yy], b2r.at[way, yy], rsem, 18 + yy, xdev(step))

    def b_three():
        for yy in range(4):
            way = 1 if yy < 2 else 0
            arrived(b2r.at[way, yy], rsem, 14 + yy, xdev(1 - 2 * way))
            arrived(b2r.at[1 - way, yy], rsem, 18 + yy, xdev(2 * way - 1))
            ub[yy] = add(ssum[2 * yy + l, HIGH, hcols(h)], b2r[0, yy], b2r[1, yy]).astype(BF16)
        far = yp(2)
        send(ub.at[far, pl.ds(0, 80)], b4r.at[pl.ds(0, 80)], rsem, 22, ydev(1))
        send(ub.at[far, pl.ds(80, 64)], b4r.at[pl.ds(80, 64)], rsem, 23, ydev(-1))

    def b_four():
        for way, (start, size) in enumerate(((0, 80), (80, 64))):
            step = 1 - 2 * way
            ds, other = pl.ds(start, size), (pl.ds(80, 64), pl.ds(0, 80))[way]
            arrived(b4r.at[ds], rsem, 22 + way, ydev(step))
            b5s[way, ds, :] = add(ub[yp(step), ds, :], b4r[ds, :]).astype(BF16)
            b5s[way, other, :] = ub[yp(step), other, :]
            send(b5s.at[way], b5r.at[way], rsem, 24 + way, ydev(step))

    def b_five():
        for way in range(2):
            arrived(b5r.at[way], rsem, 24 + way, ydev(1 - 2 * way))
        total = add(ub[y], b5r[0], b5r[1])
        outt_ref[144:288, :] = total[:, :256]
        val_ref[144:288, :] = total[:, 256:]

    X, G, OWN, OTHER = 0, 1, 0, 1
    ex_send(0, x_ref.at[oh])
    local[0].wait()
    ag_send(X, OWN, 1)
    ex_send(1, gsend)
    ag_send(G, OWN, 1)
    w_first(0)
    ex_send(2, q_ref.at[oh])
    ex_send(3, k_ref.at[oh])
    w_first(1)
    local[1].wait()
    local[2].wait()
    ag_next(X, OWN, 1)
    ex_wait(0)
    ag_send(X, OTHER, 1)
    softmax(h)
    ag_next(X, OWN, 2)
    w_second(0)
    ag_next(X, OTHER, 1)
    ag_next(G, OWN, 1)
    ag_next(X, OWN, 3)
    w_third(0)
    ag_next(X, OTHER, 2)
    ex_wait(1)
    ag_send(G, OTHER, 1)
    w_second(1)
    ex_wait(2)
    ex_wait(3)
    softmax(oh)
    w_fourth(0)
    ag_next(X, OTHER, 3)
    ag_next(G, OWN, 2)
    ag_wait(X, OWN, 4)
    transpose_half(xall, xt, OWN)
    w_third(1)
    ag_next(G, OTHER, 1)
    w_last(0)
    local[3].wait()
    values(OWN)
    ag_next(G, OWN, 3)
    w_fourth(1)
    ag_next(G, OTHER, 2)
    ag_wait(X, OTHER, 4)
    transpose_half(xall, xt, OTHER)
    values(OTHER)
    ag_next(G, OTHER, 3)
    contexts()
    wv_turn()
    w_last(1)
    local[4].wait()
    ag_wait(G, OWN, 4)
    transpose_half(gall, gt, OWN)
    grad_contexts(OWN)
    x_gram()
    ag_wait(G, OTHER, 4)
    transpose_half(gall, gt, OTHER)
    grad_contexts(OTHER)
    grad_values()
    dx_partial(OTHER)
    z_step(OTHER, 1)
    norm_send()
    dx_partial(OWN)
    z_step(OWN, 1)
    z_step(OTHER, 2)
    factor = norm_wait()
    z_step(OWN, 2)

    def first(n, carry):
        core_send(n, factor)
        return carry

    def second(n, carry):
        core_sum(n, factor)
        return carry

    lax.fori_loop(0, 8, first, 0)
    z_step(OTHER, 3)
    lax.fori_loop(0, 8, second, 0)
    a_one()
    b_one()
    z_step(OWN, 3)
    a_two()
    b_two()
    z_step(OTHER, 4)
    z_step(OWN, 4)
    a_three()
    b_three()
    a_four()
    b_four()
    gis[...] = z_final(OTHER)
    ex_send(4, gis)
    a_five()
    b_five()
    gi_ref[h] = z_final(OWN)
    ex_wait(4)
    gi_ref[oh] = gir[...]
    for copy in sent:
        copy.wait_send()


def per_device(layer_input, out_grad, loss_weight, queries, keys, value_weight, output_weight, lengths):
    any_spec = pl.BlockSpec(memory_space=pl.ANY)
    smem = pl.BlockSpec(memory_space=pltpu.SMEM)
    vmem = pl.BlockSpec(memory_space=pltpu.VMEM)

    def buf(*shape, dtype=BF16):
        return pltpu.VMEM(shape, dtype)

    dma = pltpu.SemaphoreType.DMA
    out_t, value, grad_input = pl.pallas_call(
        kernel,
        out_shape=(
            jax.ShapeDtypeStruct((288, 256), F32),
            jax.ShapeDtypeStruct((288, 128), F32),
            jax.ShapeDtypeStruct((2, TOK, D), BF16),
        ),
        in_specs=[smem, smem, any_spec, vmem, any_spec, any_spec, any_spec, any_spec],
        out_specs=(vmem, vmem, vmem),
        scratch_shapes=[
            buf(SEQ, D), buf(SEQ, D), buf(D, SEQ), buf(D, SEQ), buf(TOK, D),
            buf(SEQ, 512), buf(SEQ, 256), buf(D, 256), buf(256, D), buf(512, D),
            buf(4, SEQ, SEQ), buf(SEQ, 256), buf(SEQ, 512), buf(512, SEQ), buf(256, SEQ), buf(SEQ, 256),
            buf(SEQ, SEQ, dtype=F32), buf(NZ, 8, 128, dtype=F32), buf(SEQ, D, dtype=F32),
            buf(16, TOK, D), buf(16, TOK, D), buf(TOK, D), buf(TOK, D),
            buf(8, 288, 768), buf(8, 288, 768), buf(8, 288, 768),
            buf(2, 144, 768), buf(2, 144, 768), buf(2, 2, 144, 768), buf(2, 144, 768),
            buf(144, 384), buf(2, 144, 384), buf(2, 144, 384),
            buf(4, 144, 384), buf(4, 144, 384), buf(2, 4, 144, 384), buf(4, 144, 384),
            buf(144, 384), buf(2, 144, 384), buf(2, 144, 384),
            dma((5,)), dma((2, 5)), dma((2, 32)), dma((2, 18)), dma((2, 7)), dma((2, 16)), dma((2, 8)),
            dma((2, 26)),
        ],
        compiler_params=pltpu.CompilerParams(
            collective_id=0, has_side_effects=True, vmem_limit_bytes=60 * 1024 * 1024
        ),
        cost_estimate=pl.CostEstimate(flops=5_000_000_000, bytes_accessed=12_000_000, transcendentals=1_000_000),
        name="clipped_grads",
    )(loss_weight, lengths, layer_input, out_grad, queries, keys, value_weight, output_weight)
    return out_t.T, value, grad_input


def solution(mesh):
    in_specs = (
        P("dp", "tensor", None),
        P("dp", "tensor", None),
        P("dp"),
        P("dp", None, "tensor"),
        P("dp", None, "tensor"),
        P(None, "tensor"),
        P("tensor", None),
        P("dp"),
    )
    out_specs = (P("tensor", "dp"), P("dp", "tensor"), P("dp", "tensor", None))
    return jax.shard_map(
        per_device, mesh=mesh, in_specs=in_specs, out_specs=out_specs, check_vma=False
    )
```

```python
import jax
import jax.numpy as jnp
from jax import lax
from jax.experimental import pallas as pl
from jax.experimental.pallas import tpu as pltpu
from jax.sharding import PartitionSpec as P

D = 4608
HQ = 32
KVH = 16
HD = 128
QPRE = 144
SOFTCAP = 50
SEQ = 256
NZ = 8
TOK = 16
HALF = D // 2
MESH = pl.DeviceIdType.MESH
F32 = jnp.float32
BF16 = jnp.bfloat16


def mo(value, multiple):
    return pl.multiple_of(value, multiple)


def dot(a, b):
    return jnp.dot(a, b, preferred_element_type=F32)


def kernel(
    lw_ref, len_ref, x_ref, g_ref, q_ref, k_ref, wv_ref, wo_ref,
    outt_ref, val_ref, gi_ref,
    xall, gall, xt4, gt4, xtp, gtp, gsend, qall, kall, wv, wo, probs, vall, call, callp, dct, dvt, dv, dvp,
    gram, xgram, nbuf, fbuf, dxf, zs, zr, gis, gir, ssum,
    a1r, a2s, a2r, ua, a4r, b1r, b2s, b2r, ub, b4r,
    lsem, xsem, agsem, wsem, nsem, zsem, csem, rsem,
):
    xt, gt = xt4.reshape(D, SEQ), gt4.reshape(D, SEQ)
    dp, tn = lax.axis_index("dp"), lax.axis_index("tensor")
    h, z = lax.div(tn, NZ), lax.rem(tn, NZ)
    y, l, c = lax.div(dp, 4), lax.rem(lax.div(dp, 2), 2), lax.rem(dp, 2)
    x = 2 * h + l
    oh = 1 - h

    def zdev(step):
        return (dp, h * NZ + lax.rem(z + step + NZ, NZ))

    def ydev(step):
        return (lax.rem(y + step + 4, 4) * 4 + l * 2 + c, tn)

    def xpos(step):
        return lax.rem(x + step + 4, 4)

    def xdev(step):
        there = xpos(step)
        return (y * 4 + lax.rem(there, 2) * 2 + c, lax.div(there, 2) * NZ + z)

    partner = (dp, oh * NZ + z)
    cross = (y * 4 + (1 - l) * 2 + c, oh * NZ + z)
    core = (dp + 1 - 2 * c, tn)

    def rows(hs, zz):
        return pl.ds(mo(hs * (NZ * TOK) + zz * TOK, TOK), TOK)

    def remote(src, dst, sem, index, device):
        return pltpu.make_async_remote_copy(
            src_ref=src, dst_ref=dst, send_sem=sem.at[0, index], recv_sem=sem.at[1, index],
            device_id=device, device_id_type=MESH,
        )

    sent = []

    def send(src, dst, sem, index, device):
        copy = remote(src, dst, sem, index, device)
        copy.start()
        sent.append(copy)

    def arrived(dst, sem, index, device):
        remote(dst, dst, sem, index, device).wait_recv()

    my_rows, other_rows = rows(h, z), rows(oh, z)
    local = [
        pltpu.make_async_copy(x_ref.at[h], xall.at[my_rows], lsem.at[0]),
        pltpu.make_async_copy(q_ref.at[h], qall.at[:, pl.ds(mo(h * 256, 256), 256)], lsem.at[1]),
        pltpu.make_async_copy(k_ref.at[h], kall.at[:, pl.ds(mo(h * 128, 128), 128)], lsem.at[2]),
        pltpu.make_async_copy(wv_ref, wv.at[:, pl.ds(mo(h * 128, 128), 128)], lsem.at[3]),
        pltpu.make_async_copy(wo_ref, wo.at[pl.ds(mo(h * 256, 256), 256)], lsem.at[4]),
    ]
    for copy in local:
        copy.start()

    barrier = pltpu.get_barrier_semaphore()
    peers = [zdev(1), zdev(-1), ydev(1), ydev(-1), xdev(1), xdev(-1), xdev(2), ydev(2), core]
    for peer in peers:
        pl.semaphore_signal(barrier, inc=1, device_id=peer, device_id_type=MESH)

    position = tn * TOK + lax.broadcasted_iota(jnp.int32, (TOK, 1), 0)

    def weighted(e):
        live = (position < len_ref[e]).astype(F32)
        return (g_ref[e].astype(F32) * lw_ref[e] * live).astype(BF16)

    gall[my_rows, :] = weighted(h)
    gsend[...] = weighted(oh)


    X, G, OWN, OTHER = 0, 1, 0, 1
    arrs = (xall, gall)

    def ag_ref(arr, part, way, k, received):
        hs = h if part == 0 else oh
        back = k if received else k - 1
        origin = lax.rem(z + (NZ - back if way == 0 else back), NZ)
        columns = slice(None)
        if k == 4:
            columns = pl.ds(0, HALF) if way == 0 else pl.ds(HALF, HALF)
        return arrs[arr].at[rows(hs, origin), columns]

    def ag_index(arr, part, way, k):
        return ((arr * 2 + part) * 2 + way) * 4 + k - 1

    def ag_send(arr, part, k):
        for way in range(2):
            ref = ag_ref(arr, part, way, k, False)
            send(ref, ref, agsem, ag_index(arr, part, way, k), zdev(1 - 2 * way))

    def ag_wait(arr, part, k):
        for way in range(2):
            arrived(ag_ref(arr, part, way, k, True), agsem, ag_index(arr, part, way, k), zdev(1 - 2 * way))

    def ag_next(arr, part, k):
        ag_wait(arr, part, k)
        ag_send(arr, part, k + 1)

    def ex_refs(k, mine):
        hs = h if mine else oh
        qcol, kcol = pl.ds(mo(hs * 256, 256), 256), pl.ds(mo(hs * 128, 128), 128)
        return (
            xall.at[rows(hs, z)], gall.at[rows(hs, z)], qall.at[:, qcol], kall.at[:, kcol],
            gir,
        )[k]

    def ex_send(k, src):
        send(src, ex_refs(k, True), xsem, k, partner)

    def ex_wait(k):
        arrived(ex_refs(k, False), xsem, k, partner)

    def w_ref(arr, hs, yy, cc, part=None):
        piece = yy * 2 + cc
        size = (D // 8, 32)[arr]
        start = piece * size
        if part is not None:
            size = size // 2
            start = start + part * size
        ds = pl.ds(mo(start, 16), size)
        if arr == 0:
            return wv.at[ds, pl.ds(mo(hs * 128, 128), 128)]
        return wo.at[pl.ds(mo(hs * 256 + start, 16), size)]

    def w_first(arr):
        piece = y * 2 + c
        size = (D // 8, 32)[arr]
        src = (wv_ref, wo_ref)[arr].at[pl.ds(mo(piece * size, 16), size)]
        send(src, w_ref(arr, h, y, c), wsem, arr * 9, cross)

    def w_core(arr, step):
        yy = lax.rem(y + step, 4)
        ref = w_ref(arr, oh, yy, c)
        send(ref, ref, wsem, arr * 9 + 5 + step, core)

    def w_second(arr):
        ref = w_ref(arr, oh, y, c)
        arrived(ref, wsem, arr * 9, cross)
        send(ref, ref, wsem, arr * 9 + 1, ydev(1))
        send(ref, ref, wsem, arr * 9 + 2, ydev(-1))
        w_core(arr, 0)

    def w_third(arr):
        low, high = lax.rem(y + 3, 4), lax.rem(y + 1, 4)
        arrived(w_ref(arr, oh, low, c), wsem, arr * 9 + 1, ydev(1))
        ref = w_ref(arr, oh, low, c, 0)
        send(ref, ref, wsem, arr * 9 + 3, ydev(1))
        arrived(w_ref(arr, oh, high, c), wsem, arr * 9 + 2, ydev(-1))
        ref = w_ref(arr, oh, high, c, 1)
        send(ref, ref, wsem, arr * 9 + 4, ydev(-1))
        w_core(arr, 3)
        w_core(arr, 1)

    def w_fourth(arr):
        far = lax.rem(y + 2, 4)
        arrived(w_ref(arr, oh, far, c, 0), wsem, arr * 9 + 3, ydev(1))
        arrived(w_ref(arr, oh, far, c, 1), wsem, arr * 9 + 4, ydev(-1))
        w_core(arr, 2)

    def w_last(arr):
        for step in range(4):
            arrived(w_ref(arr, oh, lax.rem(y + step, 4), 1 - c), wsem, arr * 9 + 5 + step, core)

    def softmax(hs):
        length = len_ref[h]
        qpos = lax.broadcasted_iota(jnp.int32, (SEQ, SEQ), 0)
        kpos = lax.broadcasted_iota(jnp.int32, (SEQ, SEQ), 1)
        allowed = (kpos <= qpos) & (kpos < length)
        keys = kall[:, pl.ds(mo(hs * 128, 128), 128)]
        for g in range(2):
            query = qall[:, pl.ds(mo(hs * 256 + g * 128, 128), 128)]
            raw = lax.dot_general(query, keys, (((1,), (1,)), ((), ())), preferred_element_type=F32)
            capped = SOFTCAP * jnp.tanh(raw * (QPRE ** -0.5 / SOFTCAP))
            expo = jnp.where(allowed, jnp.exp(capped), 0.0)
            total = jnp.sum(expo, axis=1, keepdims=True)
            probs[hs * 2 + g] = (expo / total).astype(BF16)

    def transpose_half(src, dst, part):
        hs = h if part == 0 else oh
        ds = pl.ds(mo(hs * 128, 128), 128)

        def step(i, carry):
            cols = pl.ds(mo(i * 512, 512), 512)
            dst[cols, ds] = src[ds, cols].T
            return carry

        lax.fori_loop(0, D // 512, step, 0)

    def values(part):
        hs = h if part == 0 else oh
        ds = pl.ds(mo(hs * 128, 128), 128)
        vall[ds, :] = dot(xall[ds, :], wv[...]).astype(BF16)

    def contexts():
        for head in range(4):
            kv = head // 2
            call[:, head * 128:(head + 1) * 128] = dot(
                probs[head], vall[:, kv * 128:(kv + 1) * 128]
            ).astype(BF16)

    def grad_contexts(part):
        hs = h if part == 0 else oh
        ds = pl.ds(mo(hs * 128, 128), 128)
        for half in range(2):
            dct[half * 256:(half + 1) * 256, ds] = dot(
                wo[half * 256:(half + 1) * 256, :], gt[:, ds]
            ).astype(BF16)

    def grad_values():
        for kv in range(2):
            both = dot(dct[kv * 256:kv * 256 + 128, :], probs[2 * kv])
            both += dot(dct[kv * 256 + 128:kv * 256 + 256, :], probs[2 * kv + 1])
            dvt[kv * 128:(kv + 1) * 128, :] = both.astype(BF16)
        dv[...] = dvt[...].T

    def nt(a, b):
        return lax.dot_general(a, b, (((1,), (1,)), ((), ())), preferred_element_type=F32)

    def g_gram():
        gram[...] = dot(gall[...], gt[...])

    def x_gram():
        ds = pl.ds(mo(h * 128, 128), 128)
        xgram[...] = nt(xall[ds, :], xall[ds, :]) * nt(dv[ds, :], dv[ds, :])

    def norm_send():
        ds = pl.ds(mo(oh * 128, 128), 128)
        column = lax.broadcasted_iota(jnp.int32, (128, SEQ), 1)
        twice = jnp.where(lax.div(column, 128) == h, 2.0, 1.0)
        rest = nt(xall[ds, :], xall[...]) * nt(dv[ds, :], dv[...]) * twice
        total = jnp.sum(nt(call[...], call[...]) * gram[...], axis=0, keepdims=True)
        total += jnp.sum(rest, axis=0, keepdims=True)
        total = jnp.sum(total, axis=1, keepdims=True)
        total += jnp.sum(jnp.sum(xgram[...], axis=0, keepdims=True), axis=1, keepdims=True)
        nbuf[z] = jnp.broadcast_to(total, (8, 128))
        for k in range(1, NZ):
            send(nbuf.at[z], nbuf.at[z], nsem, k - 1, zdev(k))

    def norm_wait():
        for k in range(1, NZ):
            arrived(nbuf.at[lax.rem(z + NZ - k, NZ)], nsem, k - 1, zdev(k))
        sq = jnp.sum(nbuf[...], axis=0)
        bound = jnp.sqrt(F32(D * (HQ + KVH) * HD))
        fbuf[0] = bound / jnp.maximum(jnp.sqrt(sq), bound)
        send(fbuf.at[0], fbuf.at[1], csem, 6, core)

    def turned_refs(arr, part):
        hs = h if part == 0 else oh
        ds = pl.ds(mo(hs * 128, 128), 128)
        mine, there = ((xt4, xtp), (gt4, gtp))[arr]
        return mine.at[:, 1 - c, :, ds], there.at[:, :, ds]

    def turned_send(arr, part):
        src, dst = turned_refs(arr, part)
        send(src, dst, csem, arr * 2 + part, core)

    def turned_wait(arr, part):
        arrived(turned_refs(arr, part)[1], csem, arr * 2 + part, core)

    def dx_partial(part):
        hs = h if part == 0 else oh
        ds = pl.ds(mo(hs * 128, 128), 128)
        for i in range(D // 512):
            cols = slice(i * 512, (i + 1) * 512)
            dxf[ds, cols] = nt(dv[ds, :], wv[cols, :])

    def z_cols(way):
        return pl.ds(0, HALF) if way == 0 else pl.ds(HALF, HALF)

    def z_index(part, way, k):
        return (part * 2 + way) * 4 + k - 1

    def z_start(part, way, k):
        index = z_index(part, way, k)
        src, dst = zs.at[index], zr.at[index]
        if k == 1:
            src, dst = src.at[:, z_cols(way)], dst.at[:, z_cols(way)]
        send(src, dst, zsem, index, zdev(1 - 2 * way))

    def z_arrived(part, way, k):
        index = z_index(part, way, k)
        dst = zr.at[index]
        if k == 1:
            dst = dst.at[:, z_cols(way)]
        arrived(dst, zsem, index, zdev(1 - 2 * way))

    def z_step(part, k):
        hs = h if part == 0 else oh
        for way in range(2):
            hops = 5 - k
            target = rows(hs, lax.rem(z + (hops if way == 0 else NZ - hops), NZ))
            index = z_index(part, way, k)
            if k == 1:
                zs[index, :, z_cols(way)] = dxf[target, z_cols(way)].astype(BF16)
            else:
                z_arrived(part, way, k - 1)
                if k == 2:
                    mine, rest = z_cols(way), z_cols(1 - way)
                    zs[index, :, mine] = (dxf[target, mine] + zr[index - 1, :, mine].astype(F32)).astype(BF16)
                    zs[index, :, rest] = dxf[target, rest].astype(BF16)
                else:
                    zs[index] = (dxf[target, :] + zr[index - 1].astype(F32)).astype(BF16)
            z_start(part, way, k)

    def z_final(part):
        hs = h if part == 0 else oh
        for way in range(2):
            z_arrived(part, way, 4)
        total = dxf[rows(hs, z), :]
        for way in range(2):
            total += zr[z_index(part, way, 4)].astype(F32)
        return total.astype(BF16)

    def block(n, factor, factorp):
        out = dot(gt4[n, c], call[...]) * factor + dot(gtp[n], callp[...]) * factorp
        value = dot(xt4[n, c], dv[...]) * factor + dot(xtp[n], dvp[...]) * factorp
        ssum[n, :, 0:256] = out[:, :256].astype(BF16)
        ssum[n, :, 256:384] = value[:, :128].astype(BF16)
        ssum[n, :, 384:640] = out[:, 256:].astype(BF16)
        ssum[n, :, 640:768] = value[:, 128:].astype(BF16)

    def add(*pieces):
        total = pieces[0].astype(F32)
        for piece in pieces[1:]:
            total += piece.astype(F32)
        return total

    LOW, HIGH = pl.ds(0, 144), pl.ds(144, 144)

    def yp(step):
        return lax.rem(y + step + 4, 4)

    def hcols(hh):
        return pl.ds(mo(hh * 384, 128), 384)

    def xhl(step):
        there = xpos(step)
        return lax.div(there, 2), lax.rem(there, 2)

    def a_one():
        far = yp(2)
        send(ssum.at[2 * far, LOW], a1r.at[0], rsem, 0, ydev(1))
        send(ssum.at[2 * far + 1, LOW], a1r.at[1], rsem, 1, ydev(-1))

    def a_direct():
        send(ssum.at[2 * yp(1) + 1, LOW], a2r.at[0, 1], rsem, 2, ydev(1))
        send(ssum.at[2 * yp(-1), LOW], a2r.at[1, 0], rsem, 3, ydev(-1))

    def a_two():
        for way in range(2):
            step = 1 - 2 * way
            arrived(a1r.at[way], rsem, way, ydev(step))
            a2s[way] = add(ssum[2 * yp(step) + way, LOW, :], a1r[way]).astype(BF16)
            send(a2s.at[way], a2r.at[way, way], rsem, 4 + way, ydev(step))

    def a_three():
        arrived(a2r.at[0, 1], rsem, 2, ydev(1))
        arrived(a2r.at[1, 0], rsem, 3, ydev(-1))
        for way in range(2):
            arrived(a2r.at[way, way], rsem, 4 + way, ydev(1 - 2 * way))
        for ll in range(2):
            ua[ll] = add(ssum[2 * y + ll, LOW, :], a2r[0, ll], a2r[1, ll]).astype(BF16)
        for k in range(1, 4):
            ph, pll = xhl(k)
            send(ua.at[pll, :, hcols(ph)], a4r.at[k - 1], rsem, 5 + k, xdev(k))

    def a_four():
        for k in range(1, 4):
            arrived(a4r.at[k - 1], rsem, 5 + k, xdev(k))
        total = add(ua[l, :, hcols(h)], a4r[0], a4r[1], a4r[2])
        outt_ref[0:144, :] = total[:, :256]
        val_ref[0:144, :] = total[:, 256:]

    def s_high(yy, ll, hh):
        return ssum.at[2 * yy + ll, HIGH, hcols(hh)]

    def b_one(yy, way):
        ph, pll = xhl(2)
        send(s_high(yy, pll, ph), b1r.at[yy], rsem, 10 + yy, xdev(1 - 2 * way))

    def b_direct(yy, way):
        ph, pll = xhl(1 - 2 * way)
        send(s_high(yy, pll, ph), b2r.at[way, yy], rsem, 14 + yy, xdev(1 - 2 * way))

    def b_two():
        for yy in range(4):
            way = 0 if yy < 2 else 1
            step = 1 - 2 * way
            ph, pll = xhl(step)
            arrived(b1r.at[yy], rsem, 10 + yy, xdev(step))
            b2s[yy] = add(ssum[2 * yy + pll, HIGH, hcols(ph)], b1r[yy]).astype(BF16)
            send(b2s.at[yy], b2r.at[way, yy], rsem, 18 + yy, xdev(step))

    def b_three():
        for yy in range(4):
            way = 1 if yy < 2 else 0
            arrived(b2r.at[way, yy], rsem, 14 + yy, xdev(1 - 2 * way))
            arrived(b2r.at[1 - way, yy], rsem, 18 + yy, xdev(2 * way - 1))
            ub[yy] = add(ssum[2 * yy + l, HIGH, hcols(h)], b2r[0, yy], b2r[1, yy]).astype(BF16)
        for k in range(1, 4):
            send(ub.at[yp(k)], b4r.at[k - 1], rsem, 21 + k, ydev(k))

    def b_four():
        for k in range(1, 4):
            arrived(b4r.at[k - 1], rsem, 21 + k, ydev(k))
        total = add(ub[y], b4r[0], b4r[1], b4r[2])
        outt_ref[144:288, :] = total[:, :256]
        val_ref[144:288, :] = total[:, 256:]

    local[1].wait()
    local[2].wait()
    softmax(h)
    pl.semaphore_wait(barrier, len(peers))
    ex_send(1, gsend)
    ag_send(G, OWN, 1)
    w_first(1)
    local[0].wait()
    ag_send(X, OWN, 1)
    ag_next(G, OWN, 1)
    ex_send(0, x_ref.at[oh])
    ex_send(2, q_ref.at[oh])
    ex_send(3, k_ref.at[oh])
    w_first(0)
    ex_wait(1)
    ag_send(G, OTHER, 1)
    ag_next(G, OWN, 2)
    w_second(1)
    ag_next(G, OTHER, 1)
    ag_next(G, OWN, 3)
    ex_wait(2)
    ex_wait(3)
    softmax(oh)
    ag_next(X, OWN, 1)
    w_third(1)
    ag_next(G, OTHER, 2)
    w_second(0)
    ex_wait(0)
    ag_send(X, OTHER, 1)
    ag_wait(G, OWN, 4)
    transpose_half(gall, gt, OWN)
    turned_send(G, OWN)
    w_fourth(1)
    ag_next(G, OTHER, 3)
    ag_next(X, OWN, 2)
    w_third(0)
    w_last(1)
    local[4].wait()
    grad_contexts(OWN)
    ag_next(X, OTHER, 1)
    w_fourth(0)
    ag_wait(G, OTHER, 4)
    transpose_half(gall, gt, OTHER)
    turned_send(G, OTHER)
    ag_next(X, OWN, 3)
    grad_contexts(OTHER)
    grad_values()
    send(dv, dvp, csem, 4, core)
    ag_next(X, OTHER, 2)
    w_last(0)
    local[3].wait()
    dx_partial(OTHER)
    z_step(OTHER, 1)
    ag_wait(X, OWN, 4)
    values(OWN)
    dx_partial(OWN)
    ag_next(X, OTHER, 3)
    z_step(OWN, 1)
    g_gram()
    x_gram()
    transpose_half(xall, xt, OWN)
    turned_send(X, OWN)
    ag_wait(X, OTHER, 4)
    values(OTHER)
    contexts()
    send(call, callp, csem, 5, core)
    norm_send()
    z_step(OTHER, 2)
    transpose_half(xall, xt, OTHER)
    turned_send(X, OTHER)
    z_step(OWN, 2)
    norm_wait()
    for arr in (G, X):
        for part in range(2):
            turned_wait(arr, part)
    arrived(dvp, csem, 4, core)
    arrived(callp, csem, 5, core)
    arrived(fbuf.at[1], csem, 6, core)
    factor, factorp = fbuf[0][0:1, 0:1], fbuf[1][0:1, 0:1]

    block(2 * yp(2) + l, factor, factorp)
    block(2 * yp(2) + 1 - l, factor, factorp)
    a_one()

    def near(yy, carry):
        block(2 * lax.rem(yy + y + 3, 4) + l, factor, factorp)
        return carry

    lax.fori_loop(0, 3, near, 0)
    for yy in range(4):
        b_one(yy, 0 if yy < 2 else 1)

    def rest(yy, carry):
        block(2 * lax.rem(yy + y + 3, 4) + 1 - l, factor, factorp)
        return carry

    lax.fori_loop(0, 3, rest, 0)
    a_direct()
    for yy in range(4):
        b_direct(yy, 1 if yy < 2 else 0)
    z_step(OTHER, 3)
    z_step(OWN, 3)
    z_step(OTHER, 4)
    a_two()
    b_two()
    z_step(OWN, 4)
    gis[...] = z_final(OTHER)
    ex_send(4, gis)
    gi_ref[h] = z_final(OWN)
    a_three()
    b_three()
    ex_wait(4)
    gi_ref[oh] = gir[...]
    a_four()
    b_four()
    for copy in sent:
        copy.wait_send()


def finish(outt_ref, val_ref, gi_ref, out_ref, value_ref, grad_ref):
    out_ref[...] = outt_ref[...].T
    value_ref[...] = val_ref[...]
    grad_ref[...] = gi_ref[...]


def per_device(layer_input, out_grad, loss_weight, queries, keys, value_weight, output_weight, lengths):
    any_spec = pl.BlockSpec(memory_space=pl.ANY)
    smem = pl.BlockSpec(memory_space=pltpu.SMEM)
    vmem = pl.BlockSpec(memory_space=pltpu.VMEM)

    def buf(*shape, dtype=BF16):
        return pltpu.VMEM(shape, dtype)

    dma = pltpu.SemaphoreType.DMA
    out_t, value, grad_input = pl.pallas_call(
        kernel,
        out_shape=(
            jax.ShapeDtypeStruct((288, 256), F32),
            jax.ShapeDtypeStruct((288, 128), F32),
            jax.ShapeDtypeStruct((2, TOK, D), BF16),
        ),
        in_specs=[smem, smem, any_spec, vmem, any_spec, any_spec, any_spec, any_spec],
        out_specs=(vmem, vmem, vmem),
        scratch_shapes=[
            buf(SEQ, D), buf(SEQ, D), buf(8, 2, 288, SEQ), buf(8, 2, 288, SEQ), buf(8, 288, SEQ), buf(8, 288, SEQ),
            buf(TOK, D), buf(SEQ, 512), buf(SEQ, 256), buf(D, 256), buf(512, D),
            buf(4, SEQ, SEQ), buf(SEQ, 256), buf(SEQ, 512), buf(SEQ, 512), buf(512, SEQ), buf(256, SEQ),
            buf(SEQ, 256), buf(SEQ, 256),
            buf(SEQ, SEQ, dtype=F32), buf(128, 128, dtype=F32), buf(NZ, 8, 128, dtype=F32), buf(2, 8, 128, dtype=F32),
            buf(SEQ, D, dtype=F32), buf(16, TOK, D), buf(16, TOK, D), buf(TOK, D), buf(TOK, D), buf(8, 288, 768),
            buf(2, 144, 768), buf(2, 144, 768), buf(2, 2, 144, 768), buf(2, 144, 768), buf(3, 144, 384),
            buf(4, 144, 384), buf(4, 144, 384), buf(2, 4, 144, 384), buf(4, 144, 384), buf(3, 144, 384),
            dma((5,)), dma((2, 5)), dma((2, 32)), dma((2, 18)), dma((2, 7)), dma((2, 16)), dma((2, 7)),
            dma((2, 25)),
        ],
        compiler_params=pltpu.CompilerParams(
            collective_id=0, has_side_effects=True, vmem_limit_bytes=60 * 1024 * 1024
        ),
        cost_estimate=pl.CostEstimate(flops=5_000_000_000, bytes_accessed=12_000_000, transcendentals=1_000_000),
        name="clipped_grads",
    )(loss_weight, lengths, layer_input, out_grad, queries, keys, value_weight, output_weight)
    return pl.pallas_call(
        finish,
        out_shape=(
            jax.ShapeDtypeStruct((256, 288), F32),
            jax.ShapeDtypeStruct((288, 128), F32),
            jax.ShapeDtypeStruct((2, TOK, D), BF16),
        ),
        in_specs=[vmem] * 3,
        out_specs=(vmem,) * 3,
        name="finish",
    )(out_t, value, grad_input)


def solution(mesh):
    in_specs = (
        P("dp", "tensor", None),
        P("dp", "tensor", None),
        P("dp"),
        P("dp", None, "tensor"),
        P("dp", None, "tensor"),
        P(None, "tensor"),
        P("tensor", None),
        P("dp"),
    )
    out_specs = (P("tensor", "dp"), P("dp", "tensor"), P("dp", "tensor", None))
    return jax.shard_map(
        per_device, mesh=mesh, in_specs=in_specs, out_specs=out_specs, check_vma=False
    )
```

```python
import jax
import jax.numpy as jnp
from jax import lax
from jax.experimental import pallas as pl
from jax.experimental.pallas import tpu as pltpu
from jax.sharding import PartitionSpec as P

D = 4608
HQ = 32
KVH = 16
HD = 128
QPRE = 144
SOFTCAP = 50
SEQ = 256
NZ = 8
TOK = 16
HALF = D // 2
MESH = pl.DeviceIdType.MESH
F32 = jnp.float32
BF16 = jnp.bfloat16


def mo(value, multiple):
    return pl.multiple_of(value, multiple)


def dot(a, b):
    return jnp.dot(a, b, preferred_element_type=F32)


def kernel(
    lw_ref, len_ref, x_ref, g_ref, q_ref, k_ref, wv_ref, wo_ref,
    outt_ref, val_ref, gi_ref,
    xall, gall, xt4, gt4, xtp, gtp, gsend, qall, kall, wv, wo, probs, vall, call, callp, dct, dvt, dv, dvp,
    gram, xgram, nbuf, dxf, zs, zr, gis, gir, ssum,
    a1r, a2s, a2r, ua, a4r, b1r, b2s, b2r, ub, b4r,
    lsem, xsem, agsem, wsem, nsem, zsem, csem, rsem,
):
    xt, gt = xt4.reshape(D, SEQ), gt4.reshape(D, SEQ)
    dp, tn = lax.axis_index("dp"), lax.axis_index("tensor")
    h, z = lax.div(tn, NZ), lax.rem(tn, NZ)
    y, l, c = lax.div(dp, 4), lax.rem(lax.div(dp, 2), 2), lax.rem(dp, 2)
    x = 2 * h + l
    oh = 1 - h

    def zdev(step):
        return (dp, h * NZ + lax.rem(z + step + NZ, NZ))

    def ydev(step):
        return (lax.rem(y + step + 4, 4) * 4 + l * 2 + c, tn)

    def xpos(step):
        return lax.rem(x + step + 4, 4)

    def xdev(step):
        there = xpos(step)
        return (y * 4 + lax.rem(there, 2) * 2 + c, lax.div(there, 2) * NZ + z)

    partner = (dp, oh * NZ + z)
    cross = (y * 4 + (1 - l) * 2 + c, oh * NZ + z)
    core = (dp + 1 - 2 * c, tn)

    def rows(hs, zz):
        return pl.ds(mo(hs * (NZ * TOK) + zz * TOK, TOK), TOK)

    def remote(src, dst, sem, index, device):
        return pltpu.make_async_remote_copy(
            src_ref=src, dst_ref=dst, send_sem=sem.at[0, index], recv_sem=sem.at[1, index],
            device_id=device, device_id_type=MESH,
        )

    sent = []

    def send(src, dst, sem, index, device):
        copy = remote(src, dst, sem, index, device)
        copy.start()
        sent.append(copy)

    def arrived(dst, sem, index, device):
        remote(dst, dst, sem, index, device).wait_recv()

    my_rows, other_rows = rows(h, z), rows(oh, z)
    local = [
        pltpu.make_async_copy(x_ref.at[h], xall.at[my_rows], lsem.at[0]),
        pltpu.make_async_copy(q_ref.at[h], qall.at[:, pl.ds(mo(h * 256, 256), 256)], lsem.at[1]),
        pltpu.make_async_copy(k_ref.at[h], kall.at[:, pl.ds(mo(h * 128, 128), 128)], lsem.at[2]),
        pltpu.make_async_copy(wv_ref, wv.at[:, pl.ds(mo(h * 128, 128), 128)], lsem.at[3]),
        pltpu.make_async_copy(wo_ref, wo.at[pl.ds(mo(h * 256, 256), 256)], lsem.at[4]),
    ]
    for copy in local:
        copy.start()

    barrier = pltpu.get_barrier_semaphore()
    peers = [zdev(1), zdev(-1), ydev(1), ydev(-1), xdev(1), xdev(-1), xdev(2), ydev(2), core]
    for peer in peers:
        pl.semaphore_signal(barrier, inc=1, device_id=peer, device_id_type=MESH)

    position = tn * TOK + lax.broadcasted_iota(jnp.int32, (TOK, 1), 0)

    def weighted(e):
        live = (position < len_ref[e]).astype(F32)
        return (g_ref[e].astype(F32) * lw_ref[e] * live).astype(BF16)

    gall[my_rows, :] = weighted(h)
    gsend[...] = weighted(oh)


    X, G, OWN, OTHER = 0, 1, 0, 1
    arrs = (xall, gall)

    def ag_ref(arr, part, way, k, received):
        hs = h if part == 0 else oh
        back = k if received else k - 1
        origin = lax.rem(z + (NZ - back if way == 0 else back), NZ)
        columns = slice(None)
        if k == 4:
            columns = pl.ds(0, HALF) if way == 0 else pl.ds(HALF, HALF)
        return arrs[arr].at[rows(hs, origin), columns]

    def ag_index(arr, part, way, k):
        return ((arr * 2 + part) * 2 + way) * 4 + k - 1

    def ag_send(arr, part, k):
        for way in range(2):
            ref = ag_ref(arr, part, way, k, False)
            send(ref, ref, agsem, ag_index(arr, part, way, k), zdev(1 - 2 * way))

    def ag_wait(arr, part, k):
        for way in range(2):
            arrived(ag_ref(arr, part, way, k, True), agsem, ag_index(arr, part, way, k), zdev(1 - 2 * way))

    def ag_next(arr, part, k):
        ag_wait(arr, part, k)
        ag_send(arr, part, k + 1)

    def ex_refs(k, mine):
        hs = h if mine else oh
        qcol, kcol = pl.ds(mo(hs * 256, 256), 256), pl.ds(mo(hs * 128, 128), 128)
        return (
            xall.at[rows(hs, z)], gall.at[rows(hs, z)], qall.at[:, qcol], kall.at[:, kcol],
            gir,
        )[k]

    def ex_send(k, src):
        send(src, ex_refs(k, True), xsem, k, partner)

    def ex_wait(k):
        arrived(ex_refs(k, False), xsem, k, partner)

    def w_ref(arr, hs, yy, cc, part=None):
        piece = yy * 2 + cc
        size = (D // 8, 32)[arr]
        start = piece * size
        if part is not None:
            size = size // 2
            start = start + part * size
        ds = pl.ds(mo(start, 16), size)
        if arr == 0:
            return wv.at[ds, pl.ds(mo(hs * 128, 128), 128)]
        return wo.at[pl.ds(mo(hs * 256 + start, 16), size)]

    def w_first(arr):
        piece = y * 2 + c
        size = (D // 8, 32)[arr]
        src = (wv_ref, wo_ref)[arr].at[pl.ds(mo(piece * size, 16), size)]
        send(src, w_ref(arr, h, y, c), wsem, arr * 9, cross)

    def w_core(arr, step):
        yy = lax.rem(y + step, 4)
        ref = w_ref(arr, oh, yy, c)
        send(ref, ref, wsem, arr * 9 + 5 + step, core)

    def w_second(arr):
        ref = w_ref(arr, oh, y, c)
        arrived(ref, wsem, arr * 9, cross)
        send(ref, ref, wsem, arr * 9 + 1, ydev(1))
        send(ref, ref, wsem, arr * 9 + 2, ydev(-1))
        w_core(arr, 0)

    def w_third(arr):
        low, high = lax.rem(y + 3, 4), lax.rem(y + 1, 4)
        arrived(w_ref(arr, oh, low, c), wsem, arr * 9 + 1, ydev(1))
        ref = w_ref(arr, oh, low, c, 0)
        send(ref, ref, wsem, arr * 9 + 3, ydev(1))
        arrived(w_ref(arr, oh, high, c), wsem, arr * 9 + 2, ydev(-1))
        ref = w_ref(arr, oh, high, c, 1)
        send(ref, ref, wsem, arr * 9 + 4, ydev(-1))
        w_core(arr, 3)
        w_core(arr, 1)

    def w_fourth(arr):
        far = lax.rem(y + 2, 4)
        arrived(w_ref(arr, oh, far, c, 0), wsem, arr * 9 + 3, ydev(1))
        arrived(w_ref(arr, oh, far, c, 1), wsem, arr * 9 + 4, ydev(-1))
        w_core(arr, 2)

    def w_last(arr):
        for step in range(4):
            arrived(w_ref(arr, oh, lax.rem(y + step, 4), 1 - c), wsem, arr * 9 + 5 + step, core)

    def softmax(hs):
        length = len_ref[h]
        qpos = lax.broadcasted_iota(jnp.int32, (SEQ, SEQ), 0)
        kpos = lax.broadcasted_iota(jnp.int32, (SEQ, SEQ), 1)
        allowed = (kpos <= qpos) & (kpos < length)
        keys = kall[:, pl.ds(mo(hs * 128, 128), 128)]
        for g in range(2):
            query = qall[:, pl.ds(mo(hs * 256 + g * 128, 128), 128)]
            raw = lax.dot_general(query, keys, (((1,), (1,)), ((), ())), preferred_element_type=F32)
            capped = SOFTCAP * jnp.tanh(raw * (QPRE ** -0.5 / SOFTCAP))
            expo = jnp.where(allowed, jnp.exp(capped), 0.0)
            total = jnp.sum(expo, axis=1, keepdims=True)
            probs[hs * 2 + g] = (expo / total).astype(BF16)

    def transpose_half(src, dst, part):
        hs = h if part == 0 else oh
        ds = pl.ds(mo(hs * 128, 128), 128)

        def step(i, carry):
            cols = pl.ds(mo(i * 512, 512), 512)
            dst[cols, ds] = src[ds, cols].T
            return carry

        lax.fori_loop(0, D // 512, step, 0)

    def values(part):
        hs = h if part == 0 else oh
        ds = pl.ds(mo(hs * 128, 128), 128)
        vall[ds, :] = dot(xall[ds, :], wv[...]).astype(BF16)

    def contexts():
        for head in range(4):
            kv = head // 2
            call[:, head * 128:(head + 1) * 128] = dot(
                probs[head], vall[:, kv * 128:(kv + 1) * 128]
            ).astype(BF16)

    def grad_contexts(part):
        hs = h if part == 0 else oh
        ds = pl.ds(mo(hs * 128, 128), 128)
        for half in range(2):
            dct[half * 256:(half + 1) * 256, ds] = dot(
                wo[half * 256:(half + 1) * 256, :], gt[:, ds]
            ).astype(BF16)

    def grad_values():
        for kv in range(2):
            both = dot(dct[kv * 256:kv * 256 + 128, :], probs[2 * kv])
            both += dot(dct[kv * 256 + 128:kv * 256 + 256, :], probs[2 * kv + 1])
            dvt[kv * 128:(kv + 1) * 128, :] = both.astype(BF16)
        dv[...] = dvt[...].T

    def nt(a, b):
        return lax.dot_general(a, b, (((1,), (1,)), ((), ())), preferred_element_type=F32)

    def g_gram():
        gram[...] = dot(gall[...], gt[...])

    def x_gram():
        ds = pl.ds(mo(h * 128, 128), 128)
        xgram[...] = nt(xall[ds, :], xall[ds, :]) * nt(dv[ds, :], dv[ds, :])

    def norm_send():
        ds = pl.ds(mo(oh * 128, 128), 128)
        column = lax.broadcasted_iota(jnp.int32, (128, SEQ), 1)
        twice = jnp.where(lax.div(column, 128) == h, 2.0, 1.0)
        rest = nt(xall[ds, :], xall[...]) * nt(dv[ds, :], dv[...]) * twice
        total = jnp.sum(nt(call[...], call[...]) * gram[...], axis=0, keepdims=True)
        total += jnp.sum(rest, axis=0, keepdims=True)
        total = jnp.sum(total, axis=1, keepdims=True)
        total += jnp.sum(jnp.sum(xgram[...], axis=0, keepdims=True), axis=1, keepdims=True)
        nbuf[c, z] = jnp.broadcast_to(total, (8, 128))
        mine = nbuf.at[c, z]
        send(mine, mine, nsem, 0, core)
        for k in range(1, NZ):
            send(mine, mine, nsem, 2 * k - 1, zdev(k))
            send(mine, mine, nsem, 2 * k, (dp + 1 - 2 * c, zdev(k)[1]))

    def norm_wait():
        arrived(nbuf.at[1 - c, z], nsem, 0, core)
        for k in range(1, NZ):
            origin = lax.rem(z + NZ - k, NZ)
            arrived(nbuf.at[c, origin], nsem, 2 * k - 1, zdev(k))
            arrived(nbuf.at[1 - c, origin], nsem, 2 * k, (dp + 1 - 2 * c, zdev(k)[1]))
        bound = jnp.sqrt(F32(D * (HQ + KVH) * HD))
        factors = []
        for cc in (c, 1 - c):
            sq = jnp.sum(nbuf[cc], axis=0)[0:1, 0:1]
            factors.append(bound / jnp.maximum(jnp.sqrt(sq), bound))
        return factors

    def turned_refs(arr, part):
        hs = h if part == 0 else oh
        ds = pl.ds(mo(hs * 128, 128), 128)
        mine, there = ((xt4, xtp), (gt4, gtp))[arr]
        return mine.at[:, 1 - c, :, ds], there.at[:, :, ds]

    def turned_send(arr, part):
        src, dst = turned_refs(arr, part)
        send(src, dst, csem, arr * 2 + part, core)

    def turned_wait(arr, part):
        arrived(turned_refs(arr, part)[1], csem, arr * 2 + part, core)

    def dx_partial(part):
        hs = h if part == 0 else oh
        ds = pl.ds(mo(hs * 128, 128), 128)
        for i in range(D // 512):
            cols = slice(i * 512, (i + 1) * 512)
            dxf[ds, cols] = nt(dv[ds, :], wv[cols, :])

    def z_cols(way):
        return pl.ds(0, HALF) if way == 0 else pl.ds(HALF, HALF)

    def z_index(part, way, k):
        return (part * 2 + way) * 4 + k - 1

    def z_start(part, way, k):
        index = z_index(part, way, k)
        src, dst = zs.at[index], zr.at[index]
        if k == 1:
            src, dst = src.at[:, z_cols(way)], dst.at[:, z_cols(way)]
        send(src, dst, zsem, index, zdev(1 - 2 * way))

    def z_arrived(part, way, k):
        index = z_index(part, way, k)
        dst = zr.at[index]
        if k == 1:
            dst = dst.at[:, z_cols(way)]
        arrived(dst, zsem, index, zdev(1 - 2 * way))

    def z_step(part, k):
        hs = h if part == 0 else oh
        for way in range(2):
            hops = 5 - k
            target = rows(hs, lax.rem(z + (hops if way == 0 else NZ - hops), NZ))
            index = z_index(part, way, k)
            if k == 1:
                zs[index, :, z_cols(way)] = dxf[target, z_cols(way)].astype(BF16)
            else:
                z_arrived(part, way, k - 1)
                if k == 2:
                    mine, rest = z_cols(way), z_cols(1 - way)
                    zs[index, :, mine] = (dxf[target, mine] + zr[index - 1, :, mine].astype(F32)).astype(BF16)
                    zs[index, :, rest] = dxf[target, rest].astype(BF16)
                else:
                    zs[index] = (dxf[target, :] + zr[index - 1].astype(F32)).astype(BF16)
            z_start(part, way, k)

    def z_final(part):
        hs = h if part == 0 else oh
        for way in range(2):
            z_arrived(part, way, 4)
        total = dxf[rows(hs, z), :]
        for way in range(2):
            total += zr[z_index(part, way, 4)].astype(F32)
        return total.astype(BF16)

    def block(yy, ll, factor, factorp):
        n = 2 * yy + ll
        out = dot(gt4[n, c], call[...]) * factor + dot(gtp[n], callp[...]) * factorp
        value = dot(xt4[n, c], dv[...]) * factor + dot(xtp[n], dvp[...]) * factorp
        ssum[ll, yy, :, 0:256] = out[:, :256].astype(BF16)
        ssum[ll, yy, :, 256:384] = value[:, :128].astype(BF16)
        ssum[ll, yy, :, 384:640] = out[:, 256:].astype(BF16)
        ssum[ll, yy, :, 640:768] = value[:, 128:].astype(BF16)

    def add(*pieces):
        total = pieces[0].astype(F32)
        for piece in pieces[1:]:
            total += piece.astype(F32)
        return total

    def yp(step):
        return lax.rem(y + step + 4, 4)

    def hcols(hh):
        return pl.ds(mo(hh * 384, 128), 384)

    def xhl(step):
        there = xpos(step)
        return lax.div(there, 2), lax.rem(there, 2)

    parts = (pl.ds(0, 80), pl.ds(80, 64))
    highs = (pl.ds(144, 80), pl.ds(224, 64))

    def a_one(q):
        far = yp(2)
        ds = parts[q]
        send(ssum.at[0, far, ds], a1r.at[0, ds], rsem, 25 * q, ydev(1))
        send(ssum.at[1, far, ds], a1r.at[1, ds], rsem, 25 * q + 1, ydev(-1))

    def a_direct(q):
        ds = parts[q]
        send(ssum.at[1, yp(1), ds], a2r.at[0, 1, ds], rsem, 25 * q + 2, ydev(1))
        send(ssum.at[0, yp(-1), ds], a2r.at[1, 0, ds], rsem, 25 * q + 3, ydev(-1))

    def a_two(q):
        ds = parts[q]
        for way in range(2):
            step = 1 - 2 * way
            arrived(a1r.at[way, ds], rsem, 25 * q + way, ydev(step))
            a2s[way, ds, :] = add(ssum[way, yp(step), ds, :], a1r[way, ds, :]).astype(BF16)
            send(a2s.at[way, ds], a2r.at[way, way, ds], rsem, 25 * q + 4 + way, ydev(step))

    def a_three(q):
        ds = parts[q]
        arrived(a2r.at[0, 1, ds], rsem, 25 * q + 2, ydev(1))
        arrived(a2r.at[1, 0, ds], rsem, 25 * q + 3, ydev(-1))
        for way in range(2):
            arrived(a2r.at[way, way, ds], rsem, 25 * q + 4 + way, ydev(1 - 2 * way))
        for ll in range(2):
            ua[ll, ds, :] = add(ssum[ll, y, ds, :], a2r[0, ll, ds, :], a2r[1, ll, ds, :]).astype(BF16)
        for k in range(1, 4):
            ph, pll = xhl(k)
            send(ua.at[pll, ds, hcols(ph)], a4r.at[k - 1, ds], rsem, 25 * q + 5 + k, xdev(k))

    def a_four(q):
        ds = parts[q]
        for k in range(1, 4):
            arrived(a4r.at[k - 1, ds], rsem, 25 * q + 5 + k, xdev(k))
        total = add(ua[l, ds, hcols(h)], a4r[0, ds, :], a4r[1, ds, :], a4r[2, ds, :])
        outt_ref[ds, :] = total[:, :256]
        val_ref[ds, :] = total[:, 256:]

    pairs = (pl.ds(0, 2), pl.ds(2, 2))

    def s_high(q, pair, ll, hh):
        return ssum.at[ll, pairs[pair], highs[q], hcols(hh)]

    def b_one(q):
        ph, pll = xhl(2)
        for way in range(2):
            send(s_high(q, way, pll, ph), b1r.at[pairs[way], parts[q]], rsem, 25 * q + 10 + way, xdev(1 - 2 * way))

    def b_direct(q):
        for way in range(2):
            ph, pll = xhl(1 - 2 * way)
            send(s_high(q, 1 - way, pll, ph), b2r.at[way, pairs[1 - way], parts[q]], rsem, 25 * q + 14 + way, xdev(1 - 2 * way))

    def b_two(q):
        ds = parts[q]
        for way in range(2):
            step = 1 - 2 * way
            ph, pll = xhl(step)
            arrived(b1r.at[pairs[way], ds], rsem, 25 * q + 10 + way, xdev(step))
            for yy in (2 * way, 2 * way + 1):
                b2s[yy, ds, :] = add(ssum[pll, yy, highs[q], hcols(ph)], b1r[yy, ds, :]).astype(BF16)
            send(b2s.at[pairs[way], ds], b2r.at[way, pairs[way], ds], rsem, 25 * q + 18 + way, xdev(step))

    def b_three(q):
        ds = parts[q]
        for way in range(2):
            arrived(b2r.at[way, pairs[1 - way], ds], rsem, 25 * q + 14 + way, xdev(1 - 2 * way))
            arrived(b2r.at[way, pairs[way], ds], rsem, 25 * q + 18 + way, xdev(1 - 2 * way))
        for yy in range(4):
            ub[yy, ds, :] = add(ssum[l, yy, highs[q], hcols(h)], b2r[0, yy, ds, :], b2r[1, yy, ds, :]).astype(BF16)
        for k in range(1, 4):
            send(ub.at[yp(k), ds], b4r.at[k - 1, ds], rsem, 25 * q + 21 + k, ydev(k))

    def b_four(q):
        ds = parts[q]
        for k in range(1, 4):
            arrived(b4r.at[k - 1, ds], rsem, 25 * q + 21 + k, ydev(k))
        total = add(ub[y, ds, :], b4r[0, ds, :], b4r[1, ds, :], b4r[2, ds, :])
        outt_ref[highs[q], :] = total[:, :256]
        val_ref[highs[q], :] = total[:, 256:]

    local[1].wait()
    local[2].wait()
    softmax(h)
    pl.semaphore_wait(barrier, len(peers))
    ex_send(1, gsend)
    ag_send(G, OWN, 1)
    w_first(1)
    local[0].wait()
    ag_send(X, OWN, 1)
    ag_next(G, OWN, 1)
    ex_send(0, x_ref.at[oh])
    ex_wait(1)
    ag_send(G, OTHER, 1)
    ag_next(G, OWN, 2)
    w_second(1)
    ag_next(G, OTHER, 1)
    w_first(0)
    ag_next(G, OWN, 3)
    ag_next(X, OWN, 1)
    w_third(1)
    ag_next(G, OTHER, 2)
    ex_wait(0)
    ag_send(X, OTHER, 1)
    ex_send(2, q_ref.at[oh])
    ex_send(3, k_ref.at[oh])
    ag_wait(G, OWN, 4)
    transpose_half(gall, gt, OWN)
    turned_send(G, OWN)
    w_fourth(1)
    w_second(0)
    ag_next(G, OTHER, 3)
    ag_next(X, OWN, 2)
    w_last(1)
    local[4].wait()
    grad_contexts(OWN)
    ag_next(X, OTHER, 1)
    w_third(0)
    ex_wait(2)
    ex_wait(3)
    softmax(oh)
    ag_wait(G, OTHER, 4)
    transpose_half(gall, gt, OTHER)
    turned_send(G, OTHER)
    ag_next(X, OWN, 3)
    grad_contexts(OTHER)
    grad_values()
    w_fourth(0)
    send(dv, dvp, csem, 4, core)
    ag_next(X, OTHER, 2)
    w_last(0)
    local[3].wait()
    dx_partial(OTHER)
    z_step(OTHER, 1)
    ag_wait(X, OWN, 4)
    values(OWN)
    dx_partial(OWN)
    ag_next(X, OTHER, 3)
    z_step(OWN, 1)
    g_gram()
    x_gram()
    transpose_half(xall, xt, OWN)
    turned_send(X, OWN)
    for part in range(2):
        turned_wait(G, part)
    z_step(OTHER, 2)
    ag_wait(X, OTHER, 4)
    values(OTHER)
    contexts()
    send(call, callp, csem, 5, core)
    norm_send()
    transpose_half(xall, xt, OTHER)
    turned_send(X, OTHER)
    z_step(OWN, 2)
    arrived(dvp, csem, 4, core)
    arrived(callp, csem, 5, core)
    for part in range(2):
        turned_wait(X, part)
    z_step(OTHER, 3)
    factor, factorp = norm_wait()

    block(yp(2), l, factor, factorp)
    block(yp(2), 1 - l, factor, factorp)
    a_one(0)
    a_one(1)

    def near(yy, carry):
        block(lax.rem(yy + y + 3, 4), l, factor, factorp)
        return carry

    lax.fori_loop(0, 3, near, 0)
    b_one(0)
    b_one(1)

    def rest(yy, carry):
        block(lax.rem(yy + y + 3, 4), 1 - l, factor, factorp)
        return carry

    lax.fori_loop(0, 3, rest, 0)
    a_direct(0)
    b_direct(0)
    z_step(OWN, 3)
    z_step(OTHER, 4)
    a_two(0)
    a_direct(1)
    b_two(0)
    b_direct(1)
    a_two(1)
    b_two(1)
    z_step(OWN, 4)
    gis[...] = z_final(OTHER)
    ex_send(4, gis)
    a_three(0)
    b_three(0)
    gi_ref[h] = z_final(OWN)
    a_three(1)
    b_three(1)
    a_four(0)
    b_four(0)
    ex_wait(4)
    gi_ref[oh] = gir[...]
    a_four(1)
    b_four(1)
    for copy in sent:
        copy.wait_send()


def finish(outt_ref, val_ref, gi_ref, out_ref, value_ref, grad_ref):
    out_ref[...] = outt_ref[...]
    value_ref[...] = val_ref[...]
    grad_ref[...] = gi_ref[...]


def per_device(layer_input, out_grad, loss_weight, queries, keys, value_weight, output_weight, lengths):
    any_spec = pl.BlockSpec(memory_space=pl.ANY)
    smem = pl.BlockSpec(memory_space=pltpu.SMEM)
    vmem = pl.BlockSpec(memory_space=pltpu.VMEM)

    def buf(*shape, dtype=BF16):
        return pltpu.VMEM(shape, dtype)

    dma = pltpu.SemaphoreType.DMA
    out_t, value, grad_input = pl.pallas_call(
        kernel,
        out_shape=(
            jax.ShapeDtypeStruct((288, 256), F32),
            jax.ShapeDtypeStruct((288, 128), F32),
            jax.ShapeDtypeStruct((2, TOK, D), BF16),
        ),
        in_specs=[smem, smem, any_spec, vmem, any_spec, any_spec, any_spec, any_spec],
        out_specs=(vmem, vmem, vmem),
        scratch_shapes=[
            buf(SEQ, D), buf(SEQ, D), buf(8, 2, 288, SEQ), buf(8, 2, 288, SEQ), buf(8, 288, SEQ), buf(8, 288, SEQ),
            buf(TOK, D), buf(SEQ, 512), buf(SEQ, 256), buf(D, 256), buf(512, D),
            buf(4, SEQ, SEQ), buf(SEQ, 256), buf(SEQ, 512), buf(SEQ, 512), buf(512, SEQ), buf(256, SEQ),
            buf(SEQ, 256), buf(SEQ, 256),
            buf(SEQ, SEQ, dtype=F32), buf(128, 128, dtype=F32), buf(2, NZ, 8, 128, dtype=F32),
            buf(SEQ, D, dtype=F32), buf(16, TOK, D), buf(16, TOK, D), buf(TOK, D), buf(TOK, D), buf(2, 4, 288, 768),
            buf(2, 144, 768), buf(2, 144, 768), buf(2, 2, 144, 768), buf(2, 144, 768), buf(3, 144, 384),
            buf(4, 144, 384), buf(4, 144, 384), buf(2, 4, 144, 384), buf(4, 144, 384), buf(3, 144, 384),
            dma((5,)), dma((2, 5)), dma((2, 32)), dma((2, 18)), dma((2, 15)), dma((2, 16)), dma((2, 6)),
            dma((2, 50)),
        ],
        compiler_params=pltpu.CompilerParams(
            collective_id=0, has_side_effects=True, vmem_limit_bytes=60 * 1024 * 1024
        ),
        cost_estimate=pl.CostEstimate(flops=5_000_000_000, bytes_accessed=12_000_000, transcendentals=1_000_000),
        name="clipped_grads",
    )(loss_weight, lengths, layer_input, out_grad, queries, keys, value_weight, output_weight)
    out_t, value, grad_input = pl.pallas_call(
        finish,
        out_shape=(
            jax.ShapeDtypeStruct((288, 256), F32),
            jax.ShapeDtypeStruct((288, 128), F32),
            jax.ShapeDtypeStruct((2, TOK, D), BF16),
        ),
        in_specs=[vmem] * 3,
        out_specs=(vmem,) * 3,
        compiler_params=pltpu.CompilerParams(vmem_limit_bytes=60 * 1024 * 1024),
        name="finish",
    )(out_t, value, grad_input)
    return out_t.T, value, grad_input


def solution(mesh):
    in_specs = (
        P("dp", "tensor", None),
        P("dp", "tensor", None),
        P("dp"),
        P("dp", None, "tensor"),
        P("dp", None, "tensor"),
        P(None, "tensor"),
        P("tensor", None),
        P("dp"),
    )
    out_specs = (P("tensor", "dp"), P("dp", "tensor"), P("dp", "tensor", None))
    return jax.shard_map(
        per_device, mesh=mesh, in_specs=in_specs, out_specs=out_specs, check_vma=False
    )
```

```python
import jax
import jax.numpy as jnp
from jax import lax
from jax.experimental import pallas as pl
from jax.experimental.pallas import tpu as pltpu
from jax.sharding import PartitionSpec as P

D = 4608
HQ = 32
KVH = 16
HD = 128
QPRE = 144
SOFTCAP = 50
SEQ = 256
NZ = 8
TOK = 16
HALF = D // 2
MESH = pl.DeviceIdType.MESH
F32 = jnp.float32
BF16 = jnp.bfloat16


def mo(value, multiple):
    return pl.multiple_of(value, multiple)


def dot(a, b):
    return jnp.dot(a, b, preferred_element_type=F32)


def kernel(
    lw_ref, len_ref, x_ref, g_ref, q_ref, k_ref, wv_ref, wo_ref,
    outt_ref, val_ref, gi_ref,
    xall, gall, xt4, gt4, xtp, gtp, gsend, qall, kall, wv, wo, probs, vall, call, callp, dct, dvt, dv, dvp,
    gram, xgram, nbuf, dxf, zs, zr, gis, gir, ssum,
    a1r, a2s, a2r, ua, a4r, b1r, b2s, b2r, ub, b4r,
    lsem, xsem, agsem, wsem, nsem, zsem, csem, rsem,
):
    xt, gt = xt4.reshape(D, SEQ), gt4.reshape(D, SEQ)
    dp, tn = lax.axis_index("dp"), lax.axis_index("tensor")
    h, z = lax.div(tn, NZ), lax.rem(tn, NZ)
    y, l, c = lax.div(dp, 4), lax.rem(lax.div(dp, 2), 2), lax.rem(dp, 2)
    x = 2 * h + l
    oh = 1 - h

    def zdev(step):
        return (dp, h * NZ + lax.rem(z + step + NZ, NZ))

    def ydev(step):
        return (lax.rem(y + step + 4, 4) * 4 + l * 2 + c, tn)

    def xpos(step):
        return lax.rem(x + step + 4, 4)

    def xdev(step):
        there = xpos(step)
        return (y * 4 + lax.rem(there, 2) * 2 + c, lax.div(there, 2) * NZ + z)

    partner = (dp, oh * NZ + z)
    cross = (y * 4 + (1 - l) * 2 + c, oh * NZ + z)
    core = (dp + 1 - 2 * c, tn)

    def rows(hs, zz):
        return pl.ds(mo(hs * (NZ * TOK) + zz * TOK, TOK), TOK)

    def remote(src, dst, sem, index, device):
        return pltpu.make_async_remote_copy(
            src_ref=src, dst_ref=dst, send_sem=sem.at[0, index], recv_sem=sem.at[1, index],
            device_id=device, device_id_type=MESH,
        )

    sent = []

    def send(src, dst, sem, index, device):
        copy = remote(src, dst, sem, index, device)
        copy.start()
        sent.append(copy)

    def arrived(dst, sem, index, device):
        remote(dst, dst, sem, index, device).wait_recv()

    my_rows, other_rows = rows(h, z), rows(oh, z)
    local = [
        pltpu.make_async_copy(x_ref.at[h], xall.at[my_rows], lsem.at[0]),
        pltpu.make_async_copy(q_ref.at[h], qall.at[:, pl.ds(mo(h * 256, 256), 256)], lsem.at[1]),
        pltpu.make_async_copy(k_ref.at[h], kall.at[:, pl.ds(mo(h * 128, 128), 128)], lsem.at[2]),
        pltpu.make_async_copy(wv_ref, wv.at[:, pl.ds(mo(h * 128, 128), 128)], lsem.at[3]),
        pltpu.make_async_copy(wo_ref, wo.at[pl.ds(mo(h * 256, 256), 256)], lsem.at[4]),
    ]
    for copy in local:
        copy.start()

    barrier = pltpu.get_barrier_semaphore()
    peers = [zdev(1), zdev(-1), ydev(1), ydev(-1), xdev(1), xdev(-1), xdev(2), ydev(2), core]
    for peer in peers:
        pl.semaphore_signal(barrier, inc=1, device_id=peer, device_id_type=MESH)

    position = tn * TOK + lax.broadcasted_iota(jnp.int32, (TOK, 1), 0)

    def weighted(e):
        live = (position < len_ref[e]).astype(F32)
        return (g_ref[e].astype(F32) * lw_ref[e] * live).astype(BF16)

    gall[my_rows, :] = weighted(h)
    gsend[...] = weighted(oh)


    X, G, OWN, OTHER = 0, 1, 0, 1
    arrs = (xall, gall)

    def ag_ref(arr, part, way, k, received):
        hs = h if part == 0 else oh
        back = k if received else k - 1
        origin = lax.rem(z + (NZ - back if way == 0 else back), NZ)
        columns = slice(None)
        if k == 4:
            columns = pl.ds(0, HALF) if way == 0 else pl.ds(HALF, HALF)
        return arrs[arr].at[rows(hs, origin), columns]

    def ag_index(arr, part, way, k):
        return ((arr * 2 + part) * 2 + way) * 4 + k - 1

    def ag_send(arr, part, k):
        for way in range(2):
            ref = ag_ref(arr, part, way, k, False)
            send(ref, ref, agsem, ag_index(arr, part, way, k), zdev(1 - 2 * way))

    def ag_wait(arr, part, k):
        for way in range(2):
            arrived(ag_ref(arr, part, way, k, True), agsem, ag_index(arr, part, way, k), zdev(1 - 2 * way))

    def ag_next(arr, part, k):
        ag_wait(arr, part, k)
        ag_send(arr, part, k + 1)

    def ex_refs(k, mine):
        hs = h if mine else oh
        qcol, kcol = pl.ds(mo(hs * 256, 256), 256), pl.ds(mo(hs * 128, 128), 128)
        return (
            xall.at[rows(hs, z)], gall.at[rows(hs, z)], qall.at[:, qcol], kall.at[:, kcol],
            gir,
        )[k]

    def ex_send(k, src):
        send(src, ex_refs(k, True), xsem, k, partner)

    def ex_wait(k):
        arrived(ex_refs(k, False), xsem, k, partner)

    def w_ref(arr, hs, yy, cc, part=None):
        piece = yy * 2 + cc
        size = (D // 8, 32)[arr]
        start = piece * size
        if part is not None:
            size = size // 2
            start = start + part * size
        ds = pl.ds(mo(start, 16), size)
        if arr == 0:
            return wv.at[ds, pl.ds(mo(hs * 128, 128), 128)]
        return wo.at[pl.ds(mo(hs * 256 + start, 16), size)]

    def w_first(arr):
        piece = y * 2 + c
        size = (D // 8, 32)[arr]
        src = (wv_ref, wo_ref)[arr].at[pl.ds(mo(piece * size, 16), size)]
        send(src, w_ref(arr, h, y, c), wsem, arr * 9, cross)

    def w_core(arr, step):
        yy = lax.rem(y + step, 4)
        ref = w_ref(arr, oh, yy, c)
        send(ref, ref, wsem, arr * 9 + 5 + step, core)

    def w_second(arr):
        ref = w_ref(arr, oh, y, c)
        arrived(ref, wsem, arr * 9, cross)
        send(ref, ref, wsem, arr * 9 + 1, ydev(1))
        send(ref, ref, wsem, arr * 9 + 2, ydev(-1))
        w_core(arr, 0)

    def w_third(arr):
        low, high = lax.rem(y + 3, 4), lax.rem(y + 1, 4)
        arrived(w_ref(arr, oh, low, c), wsem, arr * 9 + 1, ydev(1))
        ref = w_ref(arr, oh, low, c, 0)
        send(ref, ref, wsem, arr * 9 + 3, ydev(1))
        arrived(w_ref(arr, oh, high, c), wsem, arr * 9 + 2, ydev(-1))
        ref = w_ref(arr, oh, high, c, 1)
        send(ref, ref, wsem, arr * 9 + 4, ydev(-1))
        w_core(arr, 3)
        w_core(arr, 1)

    def w_fourth(arr):
        far = lax.rem(y + 2, 4)
        arrived(w_ref(arr, oh, far, c, 0), wsem, arr * 9 + 3, ydev(1))
        arrived(w_ref(arr, oh, far, c, 1), wsem, arr * 9 + 4, ydev(-1))
        w_core(arr, 2)

    def w_last(arr):
        for step in range(4):
            arrived(w_ref(arr, oh, lax.rem(y + step, 4), 1 - c), wsem, arr * 9 + 5 + step, core)

    def softmax(hs):
        length = len_ref[h]
        qpos = lax.broadcasted_iota(jnp.int32, (SEQ, SEQ), 0)
        kpos = lax.broadcasted_iota(jnp.int32, (SEQ, SEQ), 1)
        allowed = (kpos <= qpos) & (kpos < length)
        keys = kall[:, pl.ds(mo(hs * 128, 128), 128)]
        for g in range(2):
            query = qall[:, pl.ds(mo(hs * 256 + g * 128, 128), 128)]
            raw = lax.dot_general(query, keys, (((1,), (1,)), ((), ())), preferred_element_type=F32)
            capped = SOFTCAP * jnp.tanh(raw * (QPRE ** -0.5 / SOFTCAP))
            expo = jnp.where(allowed, jnp.exp(capped), 0.0)
            total = jnp.sum(expo, axis=1, keepdims=True)
            probs[hs * 2 + g] = (expo / total).astype(BF16)

    def transpose_half(src, dst, part):
        hs = h if part == 0 else oh
        ds = pl.ds(mo(hs * 128, 128), 128)

        def step(i, carry):
            cols = pl.ds(mo(i * 512, 512), 512)
            dst[cols, ds] = src[ds, cols].T
            return carry

        lax.fori_loop(0, D // 512, step, 0)

    def values(part):
        hs = h if part == 0 else oh
        ds = pl.ds(mo(hs * 128, 128), 128)
        vall[ds, :] = dot(xall[ds, :], wv[...]).astype(BF16)

    def contexts():
        for head in range(4):
            kv = head // 2
            call[:, head * 128:(head + 1) * 128] = dot(
                probs[head], vall[:, kv * 128:(kv + 1) * 128]
            ).astype(BF16)

    def grad_contexts(part):
        hs = h if part == 0 else oh
        ds = pl.ds(mo(hs * 128, 128), 128)
        for half in range(2):
            dct[half * 256:(half + 1) * 256, ds] = dot(
                wo[half * 256:(half + 1) * 256, :], gt[:, ds]
            ).astype(BF16)

    def grad_values():
        for kv in range(2):
            both = dot(dct[kv * 256:kv * 256 + 128, :], probs[2 * kv])
            both += dot(dct[kv * 256 + 128:kv * 256 + 256, :], probs[2 * kv + 1])
            dvt[kv * 128:(kv + 1) * 128, :] = both.astype(BF16)
        dv[...] = dvt[...].T

    def nt(a, b):
        return lax.dot_general(a, b, (((1,), (1,)), ((), ())), preferred_element_type=F32)

    def g_gram():
        gram[...] = dot(gall[...], gt[...])

    def x_gram():
        ds = pl.ds(mo(h * 128, 128), 128)
        xgram[...] = nt(xall[ds, :], xall[ds, :]) * nt(dv[ds, :], dv[ds, :])

    def norm_send():
        ds = pl.ds(mo(oh * 128, 128), 128)
        column = lax.broadcasted_iota(jnp.int32, (128, SEQ), 1)
        twice = jnp.where(lax.div(column, 128) == h, 2.0, 1.0)
        rest = nt(xall[ds, :], xall[...]) * nt(dv[ds, :], dv[...]) * twice
        total = jnp.sum(nt(call[...], call[...]) * gram[...], axis=0, keepdims=True)
        total += jnp.sum(rest, axis=0, keepdims=True)
        total = jnp.sum(total, axis=1, keepdims=True)
        total += jnp.sum(jnp.sum(xgram[...], axis=0, keepdims=True), axis=1, keepdims=True)
        nbuf[c, z] = jnp.broadcast_to(total, (1, 128))
        mine = nbuf.at[c, z]
        send(mine, mine, nsem, 0, core)
        for k in (4, 3, 5, 2, 6, 1, 7):
            send(mine, mine, nsem, 2 * k - 1, zdev(k))
            send(mine, mine, nsem, 2 * k, (dp + 1 - 2 * c, zdev(k)[1]))

    def norm_wait():
        arrived(nbuf.at[1 - c, z], nsem, 0, core)
        for k in range(1, NZ):
            origin = lax.rem(z + NZ - k, NZ)
            arrived(nbuf.at[c, origin], nsem, 2 * k - 1, zdev(k))
            arrived(nbuf.at[1 - c, origin], nsem, 2 * k, (dp + 1 - 2 * c, zdev(k)[1]))
        bound = jnp.sqrt(F32(D * (HQ + KVH) * HD))
        factors = []
        for cc in (c, 1 - c):
            sq = jnp.sum(nbuf[cc], axis=0)[0:1, 0:1]
            factors.append(bound / jnp.maximum(jnp.sqrt(sq), bound))
        return factors

    def turned_refs(arr, part):
        hs = h if part == 0 else oh
        ds = pl.ds(mo(hs * 128, 128), 128)
        mine, there = ((xt4, xtp), (gt4, gtp))[arr]
        return mine.at[:, 1 - c, :, ds], there.at[:, :, ds]

    def turned_send(arr, part):
        src, dst = turned_refs(arr, part)
        send(src, dst, csem, arr * 2 + part, core)

    def turned_wait(arr, part):
        arrived(turned_refs(arr, part)[1], csem, arr * 2 + part, core)

    def dx_partial(part):
        hs = h if part == 0 else oh
        ds = pl.ds(mo(hs * 128, 128), 128)
        for i in range(D // 512):
            cols = slice(i * 512, (i + 1) * 512)
            dxf[ds, cols] = nt(dv[ds, :], wv[cols, :])

    def z_cols(way):
        return pl.ds(0, HALF) if way == 0 else pl.ds(HALF, HALF)

    def z_index(part, way, k):
        return (part * 2 + way) * 4 + k - 1

    def z_start(part, way, k):
        index = z_index(part, way, k)
        src, dst = zs.at[index], zr.at[index]
        if k == 1:
            src, dst = src.at[:, z_cols(way)], dst.at[:, z_cols(way)]
        send(src, dst, zsem, index, zdev(1 - 2 * way))

    def z_arrived(part, way, k):
        index = z_index(part, way, k)
        dst = zr.at[index]
        if k == 1:
            dst = dst.at[:, z_cols(way)]
        arrived(dst, zsem, index, zdev(1 - 2 * way))

    def z_step(part, k):
        hs = h if part == 0 else oh
        for way in range(2):
            hops = 5 - k
            target = rows(hs, lax.rem(z + (hops if way == 0 else NZ - hops), NZ))
            index = z_index(part, way, k)
            if k == 1:
                zs[index, :, z_cols(way)] = dxf[target, z_cols(way)].astype(BF16)
            else:
                z_arrived(part, way, k - 1)
                if k == 2:
                    mine, rest = z_cols(way), z_cols(1 - way)
                    zs[index, :, mine] = (dxf[target, mine] + zr[index - 1, :, mine].astype(F32)).astype(BF16)
                    zs[index, :, rest] = dxf[target, rest].astype(BF16)
                else:
                    zs[index] = (dxf[target, :] + zr[index - 1].astype(F32)).astype(BF16)
            z_start(part, way, k)

    def z_final(part):
        hs = h if part == 0 else oh
        for way in range(2):
            z_arrived(part, way, 4)
        total = dxf[rows(hs, z), :]
        for way in range(2):
            total += zr[z_index(part, way, 4)].astype(F32)
        return total.astype(BF16)

    def block(yy, ll, factor, factorp):
        n = 2 * yy + ll
        out = dot(gt4[n, c], call[...]) * factor + dot(gtp[n], callp[...]) * factorp
        value = dot(xt4[n, c], dv[...]) * factor + dot(xtp[n], dvp[...]) * factorp
        ssum[ll, yy, :, 0:256] = out[:, :256].astype(BF16)
        ssum[ll, yy, :, 256:384] = value[:, :128].astype(BF16)
        ssum[ll, yy, :, 384:640] = out[:, 256:].astype(BF16)
        ssum[ll, yy, :, 640:768] = value[:, 128:].astype(BF16)

    def add(*pieces):
        total = pieces[0].astype(F32)
        for piece in pieces[1:]:
            total += piece.astype(F32)
        return total

    def yp(step):
        return lax.rem(y + step + 4, 4)

    def hcols(hh):
        return pl.ds(mo(hh * 384, 128), 384)

    def xhl(step):
        there = xpos(step)
        return lax.div(there, 2), lax.rem(there, 2)

    parts = (pl.ds(0, 80), pl.ds(80, 80))
    bparts = (pl.ds(0, 64), pl.ds(64, 64))
    highs = (pl.ds(160, 64), pl.ds(224, 64))

    def a_one(q):
        far = yp(2)
        ds = parts[q]
        send(ssum.at[0, far, ds], a1r.at[0, ds], rsem, 25 * q, ydev(1))
        send(ssum.at[1, far, ds], a1r.at[1, ds], rsem, 25 * q + 1, ydev(-1))

    def a_direct(q):
        ds = parts[q]
        send(ssum.at[1, yp(1), ds], a2r.at[0, 1, ds], rsem, 25 * q + 2, ydev(1))
        send(ssum.at[0, yp(-1), ds], a2r.at[1, 0, ds], rsem, 25 * q + 3, ydev(-1))

    def a_two(q):
        ds = parts[q]
        for way in range(2):
            step = 1 - 2 * way
            arrived(a1r.at[way, ds], rsem, 25 * q + way, ydev(step))
            a2s[way, ds, :] = add(ssum[way, yp(step), ds, :], a1r[way, ds, :]).astype(BF16)
            send(a2s.at[way, ds], a2r.at[way, way, ds], rsem, 25 * q + 4 + way, ydev(step))

    def a_three(q):
        ds = parts[q]
        arrived(a2r.at[0, 1, ds], rsem, 25 * q + 2, ydev(1))
        arrived(a2r.at[1, 0, ds], rsem, 25 * q + 3, ydev(-1))
        for way in range(2):
            arrived(a2r.at[way, way, ds], rsem, 25 * q + 4 + way, ydev(1 - 2 * way))
        for ll in range(2):
            ua[ll, ds, :] = add(ssum[ll, y, ds, :], a2r[0, ll, ds, :], a2r[1, ll, ds, :]).astype(BF16)
        for k in range(1, 4):
            ph, pll = xhl(k)
            send(ua.at[pll, ds, hcols(ph)], a4r.at[k - 1, ds], rsem, 25 * q + 5 + k, xdev(k))

    def a_four(q):
        ds = parts[q]
        for k in range(1, 4):
            arrived(a4r.at[k - 1, ds], rsem, 25 * q + 5 + k, xdev(k))
        total = add(ua[l, ds, hcols(h)], a4r[0, ds, :], a4r[1, ds, :], a4r[2, ds, :])
        outt_ref[ds, :] = total[:, :256]
        val_ref[ds, :] = total[:, 256:]

    pairs = (pl.ds(0, 2), pl.ds(2, 2))

    def s_high(q, pair, ll, hh):
        return ssum.at[ll, pairs[pair], highs[q], hcols(hh)]

    def b_one(q):
        ph, pll = xhl(2)
        for way in range(2):
            send(s_high(q, way, pll, ph), b1r.at[pairs[way], bparts[q]], rsem, 25 * q + 10 + way, xdev(1 - 2 * way))

    def b_direct(q):
        for way in range(2):
            ph, pll = xhl(1 - 2 * way)
            send(s_high(q, 1 - way, pll, ph), b2r.at[way, pairs[1 - way], bparts[q]], rsem, 25 * q + 14 + way, xdev(1 - 2 * way))

    def b_two(q):
        ds = bparts[q]
        for way in range(2):
            step = 1 - 2 * way
            ph, pll = xhl(step)
            arrived(b1r.at[pairs[way], ds], rsem, 25 * q + 10 + way, xdev(step))
            for yy in (2 * way, 2 * way + 1):
                b2s[yy, ds, :] = add(ssum[pll, yy, highs[q], hcols(ph)], b1r[yy, ds, :]).astype(BF16)
            send(b2s.at[pairs[way], ds], b2r.at[way, pairs[way], ds], rsem, 25 * q + 18 + way, xdev(step))

    def b_three(q):
        ds = bparts[q]
        for way in range(2):
            arrived(b2r.at[way, pairs[1 - way], ds], rsem, 25 * q + 14 + way, xdev(1 - 2 * way))
            arrived(b2r.at[way, pairs[way], ds], rsem, 25 * q + 18 + way, xdev(1 - 2 * way))
        for yy in range(4):
            ub[yy, ds, :] = add(ssum[l, yy, highs[q], hcols(h)], b2r[0, yy, ds, :], b2r[1, yy, ds, :]).astype(BF16)
        for k in range(1, 4):
            send(ub.at[yp(k), ds], b4r.at[k - 1, ds], rsem, 25 * q + 21 + k, ydev(k))

    def b_four(q):
        ds = bparts[q]
        for k in range(1, 4):
            arrived(b4r.at[k - 1, ds], rsem, 25 * q + 21 + k, ydev(k))
        total = add(ub[y, ds, :], b4r[0, ds, :], b4r[1, ds, :], b4r[2, ds, :])
        outt_ref[highs[q], :] = total[:, :256]
        val_ref[highs[q], :] = total[:, 256:]

    local[1].wait()
    local[2].wait()
    softmax(h)
    pl.semaphore_wait(barrier, len(peers))
    ex_send(1, gsend)
    ag_send(G, OWN, 1)
    w_first(1)
    local[0].wait()
    ag_send(X, OWN, 1)
    ag_next(G, OWN, 1)
    ex_send(0, x_ref.at[oh])
    ex_wait(1)
    ag_send(G, OTHER, 1)
    ag_next(G, OWN, 2)
    w_second(1)
    ag_next(G, OTHER, 1)
    w_first(0)
    ag_next(G, OWN, 3)
    ag_next(X, OWN, 1)
    w_third(1)
    ag_next(G, OTHER, 2)
    ex_wait(0)
    ag_send(X, OTHER, 1)
    ex_send(2, q_ref.at[oh])
    ex_send(3, k_ref.at[oh])
    ag_wait(G, OWN, 4)
    transpose_half(gall, gt, OWN)
    turned_send(G, OWN)
    w_fourth(1)
    w_second(0)
    ag_next(G, OTHER, 3)
    ag_next(X, OWN, 2)
    w_last(1)
    local[4].wait()
    grad_contexts(OWN)
    ag_next(X, OTHER, 1)
    w_third(0)
    ex_wait(2)
    ex_wait(3)
    softmax(oh)
    ag_wait(G, OTHER, 4)
    transpose_half(gall, gt, OTHER)
    turned_send(G, OTHER)
    ag_next(X, OWN, 3)
    grad_contexts(OTHER)
    grad_values()
    w_fourth(0)
    send(dv, dvp, csem, 4, core)
    ag_next(X, OTHER, 2)
    w_last(0)
    local[3].wait()
    dx_partial(OTHER)
    ag_wait(X, OWN, 4)
    values(OWN)
    dx_partial(OWN)
    ag_next(X, OTHER, 3)
    z_step(OTHER, 1)
    z_step(OWN, 1)
    g_gram()
    x_gram()
    transpose_half(xall, xt, OWN)
    turned_send(X, OWN)
    for part in range(2):
        turned_wait(G, part)
    ag_wait(X, OTHER, 4)
    values(OTHER)
    contexts()
    send(call, callp, csem, 5, core)
    norm_send()
    z_step(OTHER, 2)
    transpose_half(xall, xt, OTHER)
    turned_send(X, OTHER)
    z_step(OWN, 2)
    arrived(dvp, csem, 4, core)
    arrived(callp, csem, 5, core)
    for part in range(2):
        turned_wait(X, part)
    z_step(OTHER, 3)
    factor, factorp = norm_wait()

    block(yp(2), l, factor, factorp)
    block(yp(2), 1 - l, factor, factorp)
    a_one(0)
    a_one(1)

    def near(yy, carry):
        block(lax.rem(yy + y + 3, 4), l, factor, factorp)
        return carry

    lax.fori_loop(0, 3, near, 0)
    b_one(0)
    b_one(1)

    def rest(yy, carry):
        block(lax.rem(yy + y + 3, 4), 1 - l, factor, factorp)
        return carry

    lax.fori_loop(0, 3, rest, 0)
    a_direct(0)
    b_direct(0)
    z_step(OWN, 3)
    a_two(0)
    a_direct(1)
    b_two(0)
    b_direct(1)
    z_step(OTHER, 4)
    a_two(1)
    b_two(1)
    a_three(0)
    b_three(0)
    z_step(OWN, 4)
    gis[...] = z_final(OTHER)
    ex_send(4, gis)
    a_three(1)
    b_three(1)
    gi_ref[h] = z_final(OWN)
    a_four(0)
    b_four(0)
    ex_wait(4)
    gi_ref[oh] = gir[...]
    a_four(1)
    b_four(1)
    for copy in sent:
        copy.wait_send()


def finish(outt_ref, val_ref, gi_ref, out_ref, value_ref, grad_ref):
    out_ref[...] = outt_ref[...]
    value_ref[...] = val_ref[...]
    grad_ref[...] = gi_ref[...]


def per_device(layer_input, out_grad, loss_weight, queries, keys, value_weight, output_weight, lengths):
    any_spec = pl.BlockSpec(memory_space=pl.ANY)
    smem = pl.BlockSpec(memory_space=pltpu.SMEM)
    vmem = pl.BlockSpec(memory_space=pltpu.VMEM)

    def buf(*shape, dtype=BF16):
        return pltpu.VMEM(shape, dtype)

    dma = pltpu.SemaphoreType.DMA
    out_t, value, grad_input = pl.pallas_call(
        kernel,
        out_shape=(
            jax.ShapeDtypeStruct((288, 256), F32),
            jax.ShapeDtypeStruct((288, 128), F32),
            jax.ShapeDtypeStruct((2, TOK, D), BF16),
        ),
        in_specs=[smem, smem, any_spec, vmem, any_spec, any_spec, any_spec, any_spec],
        out_specs=(vmem, vmem, vmem),
        scratch_shapes=[
            buf(SEQ, D), buf(SEQ, D), buf(8, 2, 288, SEQ), buf(8, 2, 288, SEQ), buf(8, 288, SEQ), buf(8, 288, SEQ),
            buf(TOK, D), buf(SEQ, 512), buf(SEQ, 256), buf(D, 256), buf(512, D),
            buf(4, SEQ, SEQ), buf(SEQ, 256), buf(SEQ, 512), buf(SEQ, 512), buf(512, SEQ), buf(256, SEQ),
            buf(SEQ, 256), buf(SEQ, 256),
            buf(SEQ, SEQ, dtype=F32), buf(128, 128, dtype=F32), buf(2, NZ, 1, 128, dtype=F32),
            buf(SEQ, D, dtype=F32), buf(16, TOK, D), buf(16, TOK, D), buf(TOK, D), buf(TOK, D), buf(2, 4, 288, 768),
            buf(2, 160, 768), buf(2, 160, 768), buf(2, 2, 160, 768), buf(2, 160, 768), buf(3, 160, 384),
            buf(4, 128, 384), buf(4, 128, 384), buf(2, 4, 128, 384), buf(4, 128, 384), buf(3, 128, 384),
            dma((5,)), dma((2, 5)), dma((2, 32)), dma((2, 18)), dma((2, 15)), dma((2, 16)), dma((2, 6)),
            dma((2, 50)),
        ],
        compiler_params=pltpu.CompilerParams(
            collective_id=0, has_side_effects=True, vmem_limit_bytes=60 * 1024 * 1024
        ),
        cost_estimate=pl.CostEstimate(flops=5_000_000_000, bytes_accessed=12_000_000, transcendentals=1_000_000),
        name="clipped_grads",
    )(loss_weight, lengths, layer_input, out_grad, queries, keys, value_weight, output_weight)
    out_t, value, grad_input = pl.pallas_call(
        finish,
        out_shape=(
            jax.ShapeDtypeStruct((288, 256), F32),
            jax.ShapeDtypeStruct((288, 128), F32),
            jax.ShapeDtypeStruct((2, TOK, D), BF16),
        ),
        in_specs=[vmem] * 3,
        out_specs=(vmem,) * 3,
        compiler_params=pltpu.CompilerParams(vmem_limit_bytes=60 * 1024 * 1024),
        name="finish",
    )(out_t, value, grad_input)
    return out_t.T, value, grad_input


def solution(mesh):
    in_specs = (
        P("dp", "tensor", None),
        P("dp", "tensor", None),
        P("dp"),
        P("dp", None, "tensor"),
        P("dp", None, "tensor"),
        P(None, "tensor"),
        P("tensor", None),
        P("dp"),
    )
    out_specs = (P("tensor", "dp"), P("dp", "tensor"), P("dp", "tensor", None))
    return jax.shard_map(
        per_device, mesh=mesh, in_specs=in_specs, out_specs=out_specs, check_vma=False
    )
```

```python
import jax
import jax.numpy as jnp
from jax import lax
from jax.experimental import pallas as pl
from jax.experimental.pallas import tpu as pltpu
from jax.sharding import PartitionSpec as P

D = 4608
HQ = 32
KVH = 16
HD = 128
QPRE = 144
SOFTCAP = 50
SEQ = 256
NZ = 8
TOK = 16
HALF = D // 2
MESH = pl.DeviceIdType.MESH
F32 = jnp.float32
BF16 = jnp.bfloat16


def mo(value, multiple):
    return pl.multiple_of(value, multiple)


def dot(a, b):
    return jnp.dot(a, b, preferred_element_type=F32)


def kernel(
    lw_ref, len_ref, x_ref, g_ref, q_ref, k_ref, wv_ref, wo_ref,
    outt_ref, val_ref, gi_ref,
    xall, gall, xt4, gt4, xtp, gtp, gsend, qall, kall, wv, wo, probs, vall, call, callp, dct, dvt, dv, dvp,
    gram, xgram, nbuf, dxf, zs, zr, gis, gir, ssum,
    a1r, a2s, a2r, ua, a4r, b1r, b2s, b2r, ub, b4r,
    lsem, xsem, agsem, wsem, nsem, zsem, csem, rsem,
):
    xt, gt = xt4.reshape(D, SEQ), gt4.reshape(D, SEQ)
    dp, tn = lax.axis_index("dp"), lax.axis_index("tensor")
    h, z = lax.div(tn, NZ), lax.rem(tn, NZ)
    y, l, c = lax.div(dp, 4), lax.rem(lax.div(dp, 2), 2), lax.rem(dp, 2)
    x = 2 * h + l
    oh = 1 - h

    def zdev(step):
        return (dp, h * NZ + lax.rem(z + step + NZ, NZ))

    def ydev(step):
        return (lax.rem(y + step + 4, 4) * 4 + l * 2 + c, tn)

    def xpos(step):
        return lax.rem(x + step + 4, 4)

    def xdev(step):
        there = xpos(step)
        return (y * 4 + lax.rem(there, 2) * 2 + c, lax.div(there, 2) * NZ + z)

    partner = (dp, oh * NZ + z)
    cross = (y * 4 + (1 - l) * 2 + c, oh * NZ + z)
    core = (dp + 1 - 2 * c, tn)

    def rows(hs, zz):
        return pl.ds(mo(hs * (NZ * TOK) + zz * TOK, TOK), TOK)

    def remote(src, dst, sem, index, device):
        return pltpu.make_async_remote_copy(
            src_ref=src, dst_ref=dst, send_sem=sem.at[0, index], recv_sem=sem.at[1, index],
            device_id=device, device_id_type=MESH,
        )

    sent = []

    def send(src, dst, sem, index, device):
        copy = remote(src, dst, sem, index, device)
        copy.start()
        sent.append(copy)

    def drain(count):
        for copy in sent[:count]:
            copy.wait_send()
        del sent[:count]

    def arrived(dst, sem, index, device):
        remote(dst, dst, sem, index, device).wait_recv()

    my_rows, other_rows = rows(h, z), rows(oh, z)
    local = [
        pltpu.make_async_copy(x_ref.at[h], xall.at[my_rows], lsem.at[0]),
        pltpu.make_async_copy(q_ref.at[h], qall.at[:, pl.ds(mo(h * 256, 256), 256)], lsem.at[1]),
        pltpu.make_async_copy(k_ref.at[h], kall.at[:, pl.ds(mo(h * 128, 128), 128)], lsem.at[2]),
        pltpu.make_async_copy(wv_ref, wv.at[:, pl.ds(mo(h * 128, 128), 128)], lsem.at[3]),
        pltpu.make_async_copy(wo_ref, wo.at[pl.ds(mo(h * 256, 256), 256)], lsem.at[4]),
    ]
    for copy in local:
        copy.start()

    barrier = pltpu.get_barrier_semaphore()
    peers = [zdev(1), zdev(-1), ydev(1), ydev(-1), xdev(1), xdev(-1), xdev(2), ydev(2), core]
    for peer in peers:
        pl.semaphore_signal(barrier, inc=1, device_id=peer, device_id_type=MESH)

    position = tn * TOK + lax.broadcasted_iota(jnp.int32, (TOK, 1), 0)

    def weighted(e):
        live = (position < len_ref[e]).astype(F32)
        return (g_ref[e].astype(F32) * lw_ref[e] * live).astype(BF16)

    gall[my_rows, :] = weighted(h)
    gsend[...] = weighted(oh)


    X, G, OWN, OTHER = 0, 1, 0, 1
    arrs = (xall, gall)

    def ag_ref(arr, part, way, k, received):
        hs = h if part == 0 else oh
        back = k if received else k - 1
        origin = lax.rem(z + (NZ - back if way == 0 else back), NZ)
        columns = slice(None)
        if k == 4:
            columns = pl.ds(0, HALF) if way == 0 else pl.ds(HALF, HALF)
        return arrs[arr].at[rows(hs, origin), columns]

    def ag_index(arr, part, way, k):
        return ((arr * 2 + part) * 2 + way) * 4 + k - 1

    def ag_send(arr, part, k):
        for way in range(2):
            ref = ag_ref(arr, part, way, k, False)
            send(ref, ref, agsem, ag_index(arr, part, way, k), zdev(1 - 2 * way))

    def ag_wait(arr, part, k):
        for way in range(2):
            arrived(ag_ref(arr, part, way, k, True), agsem, ag_index(arr, part, way, k), zdev(1 - 2 * way))

    def ag_next(arr, part, k):
        ag_wait(arr, part, k)
        ag_send(arr, part, k + 1)

    def ex_refs(k, mine):
        hs = h if mine else oh
        qcol, kcol = pl.ds(mo(hs * 256, 256), 256), pl.ds(mo(hs * 128, 128), 128)
        return (
            xall.at[rows(hs, z)], gall.at[rows(hs, z)], qall.at[:, qcol], kall.at[:, kcol],
            gir,
        )[k]

    def ex_send(k, src):
        send(src, ex_refs(k, True), xsem, k, partner)

    def ex_wait(k):
        arrived(ex_refs(k, False), xsem, k, partner)

    def w_ref(arr, hs, yy, cc, part=None):
        piece = yy * 2 + cc
        size = (D // 8, 32)[arr]
        start = piece * size
        if part is not None:
            size = size // 2
            start = start + part * size
        ds = pl.ds(mo(start, 16), size)
        if arr == 0:
            return wv.at[ds, pl.ds(mo(hs * 128, 128), 128)]
        return wo.at[pl.ds(mo(hs * 256 + start, 16), size)]

    def w_first(arr):
        piece = y * 2 + c
        size = (D // 8, 32)[arr]
        src = (wv_ref, wo_ref)[arr].at[pl.ds(mo(piece * size, 16), size)]
        send(src, w_ref(arr, h, y, c), wsem, arr * 9, cross)

    def w_core(arr, step):
        yy = lax.rem(y + step, 4)
        ref = w_ref(arr, oh, yy, c)
        send(ref, ref, wsem, arr * 9 + 5 + step, core)

    def w_second(arr):
        ref = w_ref(arr, oh, y, c)
        arrived(ref, wsem, arr * 9, cross)
        send(ref, ref, wsem, arr * 9 + 1, ydev(1))
        send(ref, ref, wsem, arr * 9 + 2, ydev(-1))
        w_core(arr, 0)

    def w_third(arr):
        low, high = lax.rem(y + 3, 4), lax.rem(y + 1, 4)
        arrived(w_ref(arr, oh, low, c), wsem, arr * 9 + 1, ydev(1))
        ref = w_ref(arr, oh, low, c, 0)
        send(ref, ref, wsem, arr * 9 + 3, ydev(1))
        arrived(w_ref(arr, oh, high, c), wsem, arr * 9 + 2, ydev(-1))
        ref = w_ref(arr, oh, high, c, 1)
        send(ref, ref, wsem, arr * 9 + 4, ydev(-1))
        w_core(arr, 3)
        w_core(arr, 1)

    def w_fourth(arr):
        far = lax.rem(y + 2, 4)
        arrived(w_ref(arr, oh, far, c, 0), wsem, arr * 9 + 3, ydev(1))
        arrived(w_ref(arr, oh, far, c, 1), wsem, arr * 9 + 4, ydev(-1))
        w_core(arr, 2)

    def w_last(arr):
        for step in range(4):
            arrived(w_ref(arr, oh, lax.rem(y + step, 4), 1 - c), wsem, arr * 9 + 5 + step, core)

    def softmax(hs):
        length = len_ref[h]
        qpos = lax.broadcasted_iota(jnp.int32, (SEQ, SEQ), 0)
        kpos = lax.broadcasted_iota(jnp.int32, (SEQ, SEQ), 1)
        allowed = (kpos <= qpos) & (kpos < length)
        keys = kall[:, pl.ds(mo(hs * 128, 128), 128)]
        for g in range(2):
            query = qall[:, pl.ds(mo(hs * 256 + g * 128, 128), 128)]
            raw = lax.dot_general(query, keys, (((1,), (1,)), ((), ())), preferred_element_type=F32)
            capped = SOFTCAP * jnp.tanh(raw * (QPRE ** -0.5 / SOFTCAP))
            expo = jnp.where(allowed, jnp.exp(capped), 0.0)
            total = jnp.sum(expo, axis=1, keepdims=True)
            probs[hs * 2 + g] = (expo / total).astype(BF16)

    def transpose_half(src, dst, part):
        hs = h if part == 0 else oh
        ds = pl.ds(mo(hs * 128, 128), 128)

        def step(i, carry):
            cols = pl.ds(mo(i * 512, 512), 512)
            dst[cols, ds] = src[ds, cols].T
            return carry

        lax.fori_loop(0, D // 512, step, 0)

    def values(part):
        hs = h if part == 0 else oh
        ds = pl.ds(mo(hs * 128, 128), 128)
        vall[ds, :] = dot(xall[ds, :], wv[...]).astype(BF16)

    def contexts():
        for head in range(4):
            kv = head // 2
            call[:, head * 128:(head + 1) * 128] = dot(
                probs[head], vall[:, kv * 128:(kv + 1) * 128]
            ).astype(BF16)

    def grad_contexts(part):
        hs = h if part == 0 else oh
        ds = pl.ds(mo(hs * 128, 128), 128)
        for half in range(2):
            dct[half * 256:(half + 1) * 256, ds] = dot(
                wo[half * 256:(half + 1) * 256, :], gt[:, ds]
            ).astype(BF16)

    def grad_values():
        for kv in range(2):
            both = dot(dct[kv * 256:kv * 256 + 128, :], probs[2 * kv])
            both += dot(dct[kv * 256 + 128:kv * 256 + 256, :], probs[2 * kv + 1])
            dvt[kv * 128:(kv + 1) * 128, :] = both.astype(BF16)
        dv[...] = dvt[...].T

    def nt(a, b):
        return lax.dot_general(a, b, (((1,), (1,)), ((), ())), preferred_element_type=F32)

    def g_gram():
        gram[...] = dot(gall[...], gt[...])

    def x_gram():
        ds = pl.ds(mo(h * 128, 128), 128)
        xgram[...] = nt(xall[ds, :], xall[ds, :]) * nt(dv[ds, :], dv[ds, :])

    def norm_send():
        ds = pl.ds(mo(oh * 128, 128), 128)
        column = lax.broadcasted_iota(jnp.int32, (128, SEQ), 1)
        twice = jnp.where(lax.div(column, 128) == h, 2.0, 1.0)
        rest = nt(xall[ds, :], xall[...]) * nt(dv[ds, :], dv[...]) * twice
        total = jnp.sum(nt(call[...], call[...]) * gram[...], axis=0, keepdims=True)
        total += jnp.sum(rest, axis=0, keepdims=True)
        total = jnp.sum(total, axis=1, keepdims=True)
        total += jnp.sum(jnp.sum(xgram[...], axis=0, keepdims=True), axis=1, keepdims=True)
        nbuf[c, z] = jnp.broadcast_to(total, (1, 128))
        mine = nbuf.at[c, z]
        send(mine, mine, nsem, 0, core)
        for k in (4, 3, 5, 2, 6, 1, 7):
            send(mine, mine, nsem, 2 * k - 1, zdev(k))
            send(mine, mine, nsem, 2 * k, (dp + 1 - 2 * c, zdev(k)[1]))

    def norm_wait():
        arrived(nbuf.at[1 - c, z], nsem, 0, core)
        for k in range(1, NZ):
            origin = lax.rem(z + NZ - k, NZ)
            arrived(nbuf.at[c, origin], nsem, 2 * k - 1, zdev(k))
            arrived(nbuf.at[1 - c, origin], nsem, 2 * k, (dp + 1 - 2 * c, zdev(k)[1]))
        bound = jnp.sqrt(F32(D * (HQ + KVH) * HD))
        factors = []
        for cc in (c, 1 - c):
            sq = jnp.sum(nbuf[cc], axis=0)[0:1, 0:1]
            factors.append(bound / jnp.maximum(jnp.sqrt(sq), bound))
        return factors

    def turned_refs(arr, part):
        hs = h if part == 0 else oh
        ds = pl.ds(mo(hs * 128, 128), 128)
        mine, there = ((xt4, xtp), (gt4, gtp))[arr]
        return mine.at[:, 1 - c, :, ds], there.at[:, :, ds]

    def turned_send(arr, part):
        src, dst = turned_refs(arr, part)
        send(src, dst, csem, arr * 2 + part, core)

    def turned_wait(arr, part):
        arrived(turned_refs(arr, part)[1], csem, arr * 2 + part, core)

    def dx_partial(part):
        hs = h if part == 0 else oh
        ds = pl.ds(mo(hs * 128, 128), 128)
        for i in range(D // 512):
            cols = slice(i * 512, (i + 1) * 512)
            dxf[ds, cols] = nt(dv[ds, :], wv[cols, :])

    def z_cols(way):
        return pl.ds(0, HALF) if way == 0 else pl.ds(HALF, HALF)

    def z_index(part, way, k):
        return (part * 2 + way) * 4 + k - 1

    def z_start(part, way, k):
        index = z_index(part, way, k)
        src, dst = zs.at[index], zr.at[index]
        if k == 1:
            src, dst = src.at[:, z_cols(way)], dst.at[:, z_cols(way)]
        send(src, dst, zsem, index, zdev(1 - 2 * way))

    def z_arrived(part, way, k):
        index = z_index(part, way, k)
        dst = zr.at[index]
        if k == 1:
            dst = dst.at[:, z_cols(way)]
        arrived(dst, zsem, index, zdev(1 - 2 * way))

    def z_step(part, k):
        hs = h if part == 0 else oh
        for way in range(2):
            hops = 5 - k
            target = rows(hs, lax.rem(z + (hops if way == 0 else NZ - hops), NZ))
            index = z_index(part, way, k)
            if k == 1:
                zs[index, :, z_cols(way)] = dxf[target, z_cols(way)].astype(BF16)
            else:
                z_arrived(part, way, k - 1)
                if k == 2:
                    mine, rest = z_cols(way), z_cols(1 - way)
                    zs[index, :, mine] = (dxf[target, mine] + zr[index - 1, :, mine].astype(F32)).astype(BF16)
                    zs[index, :, rest] = dxf[target, rest].astype(BF16)
                else:
                    zs[index] = (dxf[target, :] + zr[index - 1].astype(F32)).astype(BF16)
            z_start(part, way, k)

    def z_final(part):
        hs = h if part == 0 else oh
        for way in range(2):
            z_arrived(part, way, 4)
        total = dxf[rows(hs, z), :]
        for way in range(2):
            total += zr[z_index(part, way, 4)].astype(F32)
        return total.astype(BF16)

    def block(yy, ll, factor, factorp):
        n = 2 * yy + ll
        out = dot(gt4[n, c], call[...]) * factor + dot(gtp[n], callp[...]) * factorp
        value = dot(xt4[n, c], dv[...]) * factor + dot(xtp[n], dvp[...]) * factorp
        ssum[ll, yy, :, 0:256] = out[:, :256].astype(BF16)
        ssum[ll, yy, :, 256:384] = value[:, :128].astype(BF16)
        ssum[ll, yy, :, 384:640] = out[:, 256:].astype(BF16)
        ssum[ll, yy, :, 640:768] = value[:, 128:].astype(BF16)

    def add(*pieces):
        total = pieces[0].astype(F32)
        for piece in pieces[1:]:
            total += piece.astype(F32)
        return total

    def yp(step):
        return lax.rem(y + step + 4, 4)

    def hcols(hh):
        return pl.ds(mo(hh * 384, 128), 384)

    def xhl(step):
        there = xpos(step)
        return lax.div(there, 2), lax.rem(there, 2)

    parts = (pl.ds(0, 80), pl.ds(80, 80))
    bparts = (pl.ds(0, 64), pl.ds(64, 64))
    highs = (pl.ds(160, 64), pl.ds(224, 64))

    def a_one(q):
        far = yp(2)
        ds = parts[q]
        send(ssum.at[0, far, ds], a1r.at[0, ds], rsem, 25 * q, ydev(1))
        send(ssum.at[1, far, ds], a1r.at[1, ds], rsem, 25 * q + 1, ydev(-1))

    def a_direct(q):
        ds = parts[q]
        send(ssum.at[1, yp(1), ds], a2r.at[0, 1, ds], rsem, 25 * q + 2, ydev(1))
        send(ssum.at[0, yp(-1), ds], a2r.at[1, 0, ds], rsem, 25 * q + 3, ydev(-1))

    def a_two(q):
        ds = parts[q]
        for way in range(2):
            step = 1 - 2 * way
            arrived(a1r.at[way, ds], rsem, 25 * q + way, ydev(step))
            a2s[way, ds, :] = add(ssum[way, yp(step), ds, :], a1r[way, ds, :]).astype(BF16)
            send(a2s.at[way, ds], a2r.at[way, way, ds], rsem, 25 * q + 4 + way, ydev(step))

    def a_three(q):
        ds = parts[q]
        arrived(a2r.at[0, 1, ds], rsem, 25 * q + 2, ydev(1))
        arrived(a2r.at[1, 0, ds], rsem, 25 * q + 3, ydev(-1))
        for way in range(2):
            arrived(a2r.at[way, way, ds], rsem, 25 * q + 4 + way, ydev(1 - 2 * way))
        for ll in range(2):
            ua[ll, ds, :] = add(ssum[ll, y, ds, :], a2r[0, ll, ds, :], a2r[1, ll, ds, :]).astype(BF16)
        for k in range(1, 4):
            ph, pll = xhl(k)
            send(ua.at[pll, ds, hcols(ph)], a4r.at[k - 1, ds], rsem, 25 * q + 5 + k, xdev(k))

    def a_four(q):
        ds = parts[q]
        for k in range(1, 4):
            arrived(a4r.at[k - 1, ds], rsem, 25 * q + 5 + k, xdev(k))
        total = add(ua[l, ds, hcols(h)], a4r[0, ds, :], a4r[1, ds, :], a4r[2, ds, :])
        outt_ref[ds, :] = total[:, :256]
        val_ref[ds, :] = total[:, 256:]

    pairs = (pl.ds(0, 2), pl.ds(2, 2))

    def s_high(q, pair, ll, hh):
        return ssum.at[ll, pairs[pair], highs[q], hcols(hh)]

    def b_one(q):
        ph, pll = xhl(2)
        for way in range(2):
            send(s_high(q, way, pll, ph), b1r.at[pairs[way], bparts[q]], rsem, 25 * q + 10 + way, xdev(1 - 2 * way))

    def b_direct(q):
        for way in range(2):
            ph, pll = xhl(1 - 2 * way)
            send(s_high(q, 1 - way, pll, ph), b2r.at[way, pairs[1 - way], bparts[q]], rsem, 25 * q + 14 + way, xdev(1 - 2 * way))

    def b_two(q):
        ds = bparts[q]
        for way in range(2):
            step = 1 - 2 * way
            ph, pll = xhl(step)
            arrived(b1r.at[pairs[way], ds], rsem, 25 * q + 10 + way, xdev(step))
            for yy in (2 * way, 2 * way + 1):
                b2s[yy, ds, :] = add(ssum[pll, yy, highs[q], hcols(ph)], b1r[yy, ds, :]).astype(BF16)
            send(b2s.at[pairs[way], ds], b2r.at[way, pairs[way], ds], rsem, 25 * q + 18 + way, xdev(step))

    def b_three(q):
        ds = bparts[q]
        for way in range(2):
            arrived(b2r.at[way, pairs[1 - way], ds], rsem, 25 * q + 14 + way, xdev(1 - 2 * way))
            arrived(b2r.at[way, pairs[way], ds], rsem, 25 * q + 18 + way, xdev(1 - 2 * way))
        for yy in range(4):
            ub[yy, ds, :] = add(ssum[l, yy, highs[q], hcols(h)], b2r[0, yy, ds, :], b2r[1, yy, ds, :]).astype(BF16)
        for k in range(1, 4):
            send(ub.at[yp(k), ds], b4r.at[k - 1, ds], rsem, 25 * q + 21 + k, ydev(k))

    def b_four(q):
        ds = bparts[q]
        for k in range(1, 4):
            arrived(b4r.at[k - 1, ds], rsem, 25 * q + 21 + k, ydev(k))
        total = add(ub[y, ds, :], b4r[0, ds, :], b4r[1, ds, :], b4r[2, ds, :])
        outt_ref[highs[q], :] = total[:, :256]
        val_ref[highs[q], :] = total[:, 256:]

    local[1].wait()
    local[2].wait()
    softmax(h)
    pl.semaphore_wait(barrier, len(peers))
    ex_send(1, gsend)
    ag_send(G, OWN, 1)
    w_first(1)
    local[0].wait()
    ag_send(X, OWN, 1)
    ag_next(G, OWN, 1)
    ex_send(0, x_ref.at[oh])
    ex_wait(1)
    ag_send(G, OTHER, 1)
    ag_next(G, OWN, 2)
    w_second(1)
    ag_next(G, OTHER, 1)
    w_first(0)
    ag_next(G, OWN, 3)
    ag_next(X, OWN, 1)
    w_third(1)
    ag_next(G, OTHER, 2)
    ex_wait(0)
    ag_send(X, OTHER, 1)
    ex_send(2, q_ref.at[oh])
    ex_send(3, k_ref.at[oh])
    ag_wait(G, OWN, 4)
    transpose_half(gall, gt, OWN)
    turned_send(G, OWN)
    w_fourth(1)
    w_second(0)
    ag_next(G, OTHER, 3)
    ag_next(X, OWN, 2)
    w_last(1)
    local[4].wait()
    grad_contexts(OWN)
    ag_next(X, OTHER, 1)
    w_third(0)
    ex_wait(2)
    ex_wait(3)
    softmax(oh)
    early = len(sent)
    ag_wait(G, OTHER, 4)
    transpose_half(gall, gt, OTHER)
    turned_send(G, OTHER)
    ag_next(X, OWN, 3)
    grad_contexts(OTHER)
    grad_values()
    w_fourth(0)
    send(dv, dvp, csem, 4, core)
    ag_next(X, OTHER, 2)
    w_last(0)
    local[3].wait()
    dx_partial(OTHER)
    ag_wait(X, OWN, 4)
    values(OWN)
    dx_partial(OWN)
    ag_next(X, OTHER, 3)
    z_step(OTHER, 1)
    z_step(OWN, 1)
    g_gram()
    x_gram()
    transpose_half(xall, xt, OWN)
    turned_send(X, OWN)
    for part in range(2):
        turned_wait(G, part)
    drain(early)
    ag_wait(X, OTHER, 4)
    gathers = len(sent)
    values(OTHER)
    contexts()
    norm_send()
    send(call, callp, csem, 5, core)
    z_step(OTHER, 2)
    transpose_half(xall, xt, OTHER)
    turned_send(X, OTHER)
    z_step(OWN, 2)
    arrived(dvp, csem, 4, core)
    arrived(callp, csem, 5, core)
    for part in range(2):
        turned_wait(X, part)
    z_step(OTHER, 3)
    drain(gathers)
    before = len(sent)
    factor, factorp = norm_wait()

    block(yp(2), l, factor, factorp)
    block(yp(2), 1 - l, factor, factorp)
    a_one(0)
    a_one(1)

    def near(yy, carry):
        block(lax.rem(yy + y + 3, 4), l, factor, factorp)
        return carry

    lax.fori_loop(0, 3, near, 0, unroll=True)
    b_one(0)
    b_one(1)

    def rest(yy, carry):
        block(lax.rem(yy + y + 3, 4), 1 - l, factor, factorp)
        return carry

    lax.fori_loop(0, 3, rest, 0, unroll=True)
    a_direct(0)
    b_direct(0)
    z_step(OWN, 3)
    a_two(0)
    a_direct(1)
    b_two(0)
    b_direct(1)
    z_step(OTHER, 4)
    a_two(1)
    b_two(1)
    drain(before)
    first = len(sent)
    a_three(0)
    b_three(0)
    z_step(OWN, 4)
    gis[...] = z_final(OTHER)
    ex_send(4, gis)
    a_three(1)
    b_three(1)
    gi_ref[h] = z_final(OWN)
    drain(first)
    a_four(0)
    b_four(0)
    a_four(1)
    b_four(1)
    ex_wait(4)
    gi_ref[oh] = gir[...]
    for copy in sent:
        copy.wait_send()


def finish(outt_ref, val_ref, gi_ref, out_ref, value_ref, grad_ref):
    out_ref[...] = outt_ref[...]
    value_ref[...] = val_ref[...]
    grad_ref[...] = gi_ref[...]


def per_device(layer_input, out_grad, loss_weight, queries, keys, value_weight, output_weight, lengths):
    any_spec = pl.BlockSpec(memory_space=pl.ANY)
    smem = pl.BlockSpec(memory_space=pltpu.SMEM)
    vmem = pl.BlockSpec(memory_space=pltpu.VMEM)

    def buf(*shape, dtype=BF16):
        return pltpu.VMEM(shape, dtype)

    dma = pltpu.SemaphoreType.DMA
    out_t, value, grad_input = pl.pallas_call(
        kernel,
        out_shape=(
            jax.ShapeDtypeStruct((288, 256), F32),
            jax.ShapeDtypeStruct((288, 128), F32),
            jax.ShapeDtypeStruct((2, TOK, D), BF16),
        ),
        in_specs=[smem, smem, any_spec, vmem, any_spec, any_spec, any_spec, any_spec],
        out_specs=(vmem, vmem, vmem),
        scratch_shapes=[
            buf(SEQ, D), buf(SEQ, D), buf(8, 2, 288, SEQ), buf(8, 2, 288, SEQ), buf(8, 288, SEQ), buf(8, 288, SEQ),
            buf(TOK, D), buf(SEQ, 512), buf(SEQ, 256), buf(D, 256), buf(512, D),
            buf(4, SEQ, SEQ), buf(SEQ, 256), buf(SEQ, 512), buf(SEQ, 512), buf(512, SEQ), buf(256, SEQ),
            buf(SEQ, 256), buf(SEQ, 256),
            buf(SEQ, SEQ, dtype=F32), buf(128, 128, dtype=F32), buf(2, NZ, 1, 128, dtype=F32),
            buf(SEQ, D, dtype=F32), buf(16, TOK, D), buf(16, TOK, D), buf(TOK, D), buf(TOK, D), buf(2, 4, 288, 768),
            buf(2, 160, 768), buf(2, 160, 768), buf(2, 2, 160, 768), buf(2, 160, 768), buf(3, 160, 384),
            buf(4, 128, 384), buf(4, 128, 384), buf(2, 4, 128, 384), buf(4, 128, 384), buf(3, 128, 384),
            dma((5,)), dma((2, 5)), dma((2, 32)), dma((2, 18)), dma((2, 15)), dma((2, 16)), dma((2, 6)),
            dma((2, 50)),
        ],
        compiler_params=pltpu.CompilerParams(
            collective_id=0, has_side_effects=True, vmem_limit_bytes=60 * 1024 * 1024
        ),
        cost_estimate=pl.CostEstimate(flops=5_000_000_000, bytes_accessed=12_000_000, transcendentals=1_000_000),
        name="clipped_grads",
    )(loss_weight, lengths, layer_input, out_grad, queries, keys, value_weight, output_weight)
    out_t, value, grad_input = pl.pallas_call(
        finish,
        out_shape=(
            jax.ShapeDtypeStruct((288, 256), F32),
            jax.ShapeDtypeStruct((288, 128), F32),
            jax.ShapeDtypeStruct((2, TOK, D), BF16),
        ),
        in_specs=[vmem] * 3,
        out_specs=(vmem,) * 3,
        compiler_params=pltpu.CompilerParams(vmem_limit_bytes=60 * 1024 * 1024),
        name="finish",
    )(out_t, value, grad_input)
    return out_t.T, value, grad_input


def solution(mesh):
    in_specs = (
        P("dp", "tensor", None),
        P("dp", "tensor", None),
        P("dp"),
        P("dp", None, "tensor"),
        P("dp", None, "tensor"),
        P(None, "tensor"),
        P("tensor", None),
        P("dp"),
    )
    out_specs = (P("tensor", "dp"), P("dp", "tensor"), P("dp", "tensor", None))
    return jax.shard_map(
        per_device, mesh=mesh, in_specs=in_specs, out_specs=out_specs, check_vma=False
    )
```

```python
import jax
import jax.numpy as jnp
from jax import lax
from jax.experimental import pallas as pl
from jax.experimental.pallas import tpu as pltpu
from jax.sharding import PartitionSpec as P

D = 4608
HQ = 32
KVH = 16
HD = 128
QPRE = 144
SOFTCAP = 50
SEQ = 256
NZ = 8
TOK = 16
HALF = D // 2
MESH = pl.DeviceIdType.MESH
F32 = jnp.float32
BF16 = jnp.bfloat16


def mo(value, multiple):
    return pl.multiple_of(value, multiple)


def dot(a, b):
    return jnp.dot(a, b, preferred_element_type=F32)


def kernel(
    lw_ref, len_ref, x_ref, g_ref, q_ref, k_ref, wv_ref, wo_ref,
    outt_ref, val_ref, gi_ref,
    xall, gall, xt4, gt4, xtp, gtp, gsend, qall, kall, wv, wo, probs, vall, call, callp, dct, dvt, dv, dvp,
    gram, xgram, nbuf, dxf, zs, zr, gis, gir, ssum,
    a1r, a2s, a2r, ua, a4r, b1r, b2s, b2r, ub, b4r,
    lsem, xsem, agsem, wsem, nsem, zsem, csem, rsem,
):
    xt, gt = xt4.reshape(D, SEQ), gt4.reshape(D, SEQ)
    dp, tn = lax.axis_index("dp"), lax.axis_index("tensor")
    h, z = lax.div(tn, NZ), lax.rem(tn, NZ)
    y, l, c = lax.div(dp, 4), lax.rem(lax.div(dp, 2), 2), lax.rem(dp, 2)
    x = 2 * h + l
    oh = 1 - h

    def zdev(step):
        return (dp, h * NZ + lax.rem(z + step + NZ, NZ))

    def ydev(step):
        return (lax.rem(y + step + 4, 4) * 4 + l * 2 + c, tn)

    def xpos(step):
        return lax.rem(x + step + 4, 4)

    def xdev(step):
        there = xpos(step)
        return (y * 4 + lax.rem(there, 2) * 2 + c, lax.div(there, 2) * NZ + z)

    partner = (dp, oh * NZ + z)
    cross = (y * 4 + (1 - l) * 2 + c, oh * NZ + z)
    core = (dp + 1 - 2 * c, tn)

    def rows(hs, zz):
        return pl.ds(mo(hs * (NZ * TOK) + zz * TOK, TOK), TOK)

    def remote(src, dst, sem, index, device):
        return pltpu.make_async_remote_copy(
            src_ref=src, dst_ref=dst, send_sem=sem.at[0, index], recv_sem=sem.at[1, index],
            device_id=device, device_id_type=MESH,
        )

    sent = []

    def send(src, dst, sem, index, device):
        copy = remote(src, dst, sem, index, device)
        copy.start()
        sent.append(copy)

    def drain(count):
        for copy in sent[:count]:
            copy.wait_send()
        del sent[:count]

    def arrived(dst, sem, index, device):
        remote(dst, dst, sem, index, device).wait_recv()

    my_rows, other_rows = rows(h, z), rows(oh, z)
    local = [
        pltpu.make_async_copy(x_ref.at[h], xall.at[my_rows], lsem.at[0]),
        pltpu.make_async_copy(q_ref.at[h], qall.at[:, pl.ds(mo(h * 256, 256), 256)], lsem.at[1]),
        pltpu.make_async_copy(k_ref.at[h], kall.at[:, pl.ds(mo(h * 128, 128), 128)], lsem.at[2]),
        pltpu.make_async_copy(wv_ref, wv.at[:, pl.ds(mo(h * 128, 128), 128)], lsem.at[3]),
        pltpu.make_async_copy(wo_ref, wo.at[pl.ds(mo(h * 256, 256), 256)], lsem.at[4]),
    ]
    for copy in local:
        copy.start()

    barrier = pltpu.get_barrier_semaphore()
    peers = [zdev(1), zdev(-1), ydev(1), ydev(-1), xdev(1), xdev(-1), xdev(2), ydev(2), core]
    for peer in peers:
        pl.semaphore_signal(barrier, inc=1, device_id=peer, device_id_type=MESH)

    position = tn * TOK + lax.broadcasted_iota(jnp.int32, (TOK, 1), 0)

    def weighted(e):
        live = (position < len_ref[e]).astype(F32)
        return (g_ref[e].astype(F32) * lw_ref[e] * live).astype(BF16)

    gall[my_rows, :] = weighted(h)
    gsend[...] = weighted(oh)


    X, G, OWN, OTHER = 0, 1, 0, 1
    arrs = (xall, gall)

    def ag_ref(arr, part, way, k, received):
        hs = h if part == 0 else oh
        back = k if received else k - 1
        origin = lax.rem(z + (NZ - back if way == 0 else back), NZ)
        columns = slice(None)
        if k == 4:
            columns = pl.ds(0, HALF) if way == 0 else pl.ds(HALF, HALF)
        return arrs[arr].at[rows(hs, origin), columns]

    def ag_index(arr, part, way, k):
        return ((arr * 2 + part) * 2 + way) * 4 + k - 1

    def ag_send(arr, part, k):
        for way in range(2):
            ref = ag_ref(arr, part, way, k, False)
            send(ref, ref, agsem, ag_index(arr, part, way, k), zdev(1 - 2 * way))

    def ag_wait(arr, part, k):
        for way in range(2):
            arrived(ag_ref(arr, part, way, k, True), agsem, ag_index(arr, part, way, k), zdev(1 - 2 * way))

    def ag_next(arr, part, k):
        ag_wait(arr, part, k)
        ag_send(arr, part, k + 1)

    def ex_refs(k, mine):
        hs = h if mine else oh
        qcol, kcol = pl.ds(mo(hs * 256, 256), 256), pl.ds(mo(hs * 128, 128), 128)
        return (
            xall.at[rows(hs, z)], gall.at[rows(hs, z)], qall.at[:, qcol], kall.at[:, kcol],
            gir,
        )[k]

    def ex_send(k, src):
        send(src, ex_refs(k, True), xsem, k, partner)

    def ex_wait(k):
        arrived(ex_refs(k, False), xsem, k, partner)

    def w_ref(arr, hs, yy, cc, part=None):
        piece = yy * 2 + cc
        size = (D // 8, 32)[arr]
        start = piece * size
        if part is not None:
            size = size // 2
            start = start + part * size
        ds = pl.ds(mo(start, 16), size)
        if arr == 0:
            return wv.at[ds, pl.ds(mo(hs * 128, 128), 128)]
        return wo.at[pl.ds(mo(hs * 256 + start, 16), size)]

    def w_first(arr):
        piece = y * 2 + c
        size = (D // 8, 32)[arr]
        src = (wv_ref, wo_ref)[arr].at[pl.ds(mo(piece * size, 16), size)]
        send(src, w_ref(arr, h, y, c), wsem, arr * 9, cross)

    def w_core(arr, step):
        yy = lax.rem(y + step, 4)
        ref = w_ref(arr, oh, yy, c)
        send(ref, ref, wsem, arr * 9 + 5 + step, core)

    def w_second(arr):
        ref = w_ref(arr, oh, y, c)
        arrived(ref, wsem, arr * 9, cross)
        send(ref, ref, wsem, arr * 9 + 1, ydev(1))
        send(ref, ref, wsem, arr * 9 + 2, ydev(-1))
        w_core(arr, 0)

    def w_third(arr):
        low, high = lax.rem(y + 3, 4), lax.rem(y + 1, 4)
        arrived(w_ref(arr, oh, low, c), wsem, arr * 9 + 1, ydev(1))
        ref = w_ref(arr, oh, low, c, 0)
        send(ref, ref, wsem, arr * 9 + 3, ydev(1))
        arrived(w_ref(arr, oh, high, c), wsem, arr * 9 + 2, ydev(-1))
        ref = w_ref(arr, oh, high, c, 1)
        send(ref, ref, wsem, arr * 9 + 4, ydev(-1))
        w_core(arr, 3)
        w_core(arr, 1)

    def w_fourth(arr):
        far = lax.rem(y + 2, 4)
        arrived(w_ref(arr, oh, far, c, 0), wsem, arr * 9 + 3, ydev(1))
        arrived(w_ref(arr, oh, far, c, 1), wsem, arr * 9 + 4, ydev(-1))
        w_core(arr, 2)

    def w_last(arr):
        for step in range(4):
            arrived(w_ref(arr, oh, lax.rem(y + step, 4), 1 - c), wsem, arr * 9 + 5 + step, core)

    def softmax(hs):
        length = len_ref[h]
        qpos = lax.broadcasted_iota(jnp.int32, (SEQ, SEQ), 0)
        kpos = lax.broadcasted_iota(jnp.int32, (SEQ, SEQ), 1)
        allowed = (kpos <= qpos) & (kpos < length)
        keys = kall[:, pl.ds(mo(hs * 128, 128), 128)]
        for g in range(2):
            query = qall[:, pl.ds(mo(hs * 256 + g * 128, 128), 128)]
            raw = lax.dot_general(query, keys, (((1,), (1,)), ((), ())), preferred_element_type=F32)
            capped = SOFTCAP * jnp.tanh(raw * (QPRE ** -0.5 / SOFTCAP))
            expo = jnp.where(allowed, jnp.exp(capped), 0.0)
            total = jnp.sum(expo, axis=1, keepdims=True)
            probs[hs * 2 + g] = (expo / total).astype(BF16)

    def transpose_half(src, dst, part):
        hs = h if part == 0 else oh
        ds = pl.ds(mo(hs * 128, 128), 128)

        def step(i, carry):
            cols = pl.ds(mo(i * 512, 512), 512)
            dst[cols, ds] = src[ds, cols].T
            return carry

        lax.fori_loop(0, D // 512, step, 0)

    def values(part):
        hs = h if part == 0 else oh
        ds = pl.ds(mo(hs * 128, 128), 128)
        vall[ds, :] = dot(xall[ds, :], wv[...]).astype(BF16)

    def contexts():
        for head in range(4):
            kv = head // 2
            call[:, head * 128:(head + 1) * 128] = dot(
                probs[head], vall[:, kv * 128:(kv + 1) * 128]
            ).astype(BF16)

    def grad_contexts(part):
        hs = h if part == 0 else oh
        ds = pl.ds(mo(hs * 128, 128), 128)
        for half in range(2):
            dct[half * 256:(half + 1) * 256, ds] = dot(
                wo[half * 256:(half + 1) * 256, :], gt[:, ds]
            ).astype(BF16)

    def grad_values():
        for kv in range(2):
            both = dot(dct[kv * 256:kv * 256 + 128, :], probs[2 * kv])
            both += dot(dct[kv * 256 + 128:kv * 256 + 256, :], probs[2 * kv + 1])
            dvt[kv * 128:(kv + 1) * 128, :] = both.astype(BF16)
        dv[...] = dvt[...].T

    def nt(a, b):
        return lax.dot_general(a, b, (((1,), (1,)), ((), ())), preferred_element_type=F32)

    def g_gram():
        gram[...] = dot(gall[...], gt[...])

    def x_gram():
        ds = pl.ds(mo(h * 128, 128), 128)
        xgram[...] = nt(xall[ds, :], xall[ds, :]) * nt(dv[ds, :], dv[ds, :])

    def norm_send():
        ds = pl.ds(mo(oh * 128, 128), 128)
        column = lax.broadcasted_iota(jnp.int32, (128, SEQ), 1)
        twice = jnp.where(lax.div(column, 128) == h, 2.0, 1.0)
        rest = nt(xall[ds, :], xall[...]) * nt(dv[ds, :], dv[...]) * twice
        total = jnp.sum(nt(call[...], call[...]) * gram[...], axis=0, keepdims=True)
        total += jnp.sum(rest, axis=0, keepdims=True)
        total = jnp.sum(total, axis=1, keepdims=True)
        total += jnp.sum(jnp.sum(xgram[...], axis=0, keepdims=True), axis=1, keepdims=True)
        nbuf[c, z] = jnp.broadcast_to(total, (1, 128))
        mine = nbuf.at[c, z]
        send(mine, mine, nsem, 0, core)
        for k in (4, 3, 5, 2, 6, 1, 7):
            send(mine, mine, nsem, 2 * k - 1, zdev(k))
            send(mine, mine, nsem, 2 * k, (dp + 1 - 2 * c, zdev(k)[1]))

    def norm_wait():
        arrived(nbuf.at[1 - c, z], nsem, 0, core)
        for k in range(1, NZ):
            origin = lax.rem(z + NZ - k, NZ)
            arrived(nbuf.at[c, origin], nsem, 2 * k - 1, zdev(k))
            arrived(nbuf.at[1 - c, origin], nsem, 2 * k, (dp + 1 - 2 * c, zdev(k)[1]))
        bound = jnp.sqrt(F32(D * (HQ + KVH) * HD))
        factors = []
        for cc in (c, 1 - c):
            sq = jnp.sum(nbuf[cc], axis=0)[0:1, 0:1]
            factors.append(bound / jnp.maximum(jnp.sqrt(sq), bound))
        return factors

    def turned_refs(arr, part):
        hs = h if part == 0 else oh
        ds = pl.ds(mo(hs * 128, 128), 128)
        mine, there = ((xt4, xtp), (gt4, gtp))[arr]
        return mine.at[:, 1 - c, :, ds], there.at[:, :, ds]

    def turned_send(arr, part):
        src, dst = turned_refs(arr, part)
        send(src, dst, csem, arr * 2 + part, core)

    def turned_wait(arr, part):
        arrived(turned_refs(arr, part)[1], csem, arr * 2 + part, core)

    def dx_partial(part):
        hs = h if part == 0 else oh
        ds = pl.ds(mo(hs * 128, 128), 128)
        for i in range(D // 512):
            cols = slice(i * 512, (i + 1) * 512)
            dxf[ds, cols] = nt(dv[ds, :], wv[cols, :])

    def z_cols(way):
        return pl.ds(0, HALF) if way == 0 else pl.ds(HALF, HALF)

    def z_index(part, way, k):
        return (part * 2 + way) * 4 + k - 1

    def z_start(part, way, k):
        index = z_index(part, way, k)
        src, dst = zs.at[index], zr.at[index]
        if k == 1:
            src, dst = src.at[:, z_cols(way)], dst.at[:, z_cols(way)]
        send(src, dst, zsem, index, zdev(1 - 2 * way))

    def z_arrived(part, way, k):
        index = z_index(part, way, k)
        dst = zr.at[index]
        if k == 1:
            dst = dst.at[:, z_cols(way)]
        arrived(dst, zsem, index, zdev(1 - 2 * way))

    def z_step(part, k):
        hs = h if part == 0 else oh
        for way in range(2):
            hops = 5 - k
            target = rows(hs, lax.rem(z + (hops if way == 0 else NZ - hops), NZ))
            index = z_index(part, way, k)
            if k == 1:
                zs[index, :, z_cols(way)] = dxf[target, z_cols(way)].astype(BF16)
            else:
                z_arrived(part, way, k - 1)
                if k == 2:
                    mine, rest = z_cols(way), z_cols(1 - way)
                    zs[index, :, mine] = (dxf[target, mine] + zr[index - 1, :, mine].astype(F32)).astype(BF16)
                    zs[index, :, rest] = dxf[target, rest].astype(BF16)
                else:
                    zs[index] = (dxf[target, :] + zr[index - 1].astype(F32)).astype(BF16)
            z_start(part, way, k)

    def z_final(part):
        hs = h if part == 0 else oh
        for way in range(2):
            z_arrived(part, way, 4)
        total = dxf[rows(hs, z), :]
        for way in range(2):
            total += zr[z_index(part, way, 4)].astype(F32)
        return total.astype(BF16)

    def block(yy, ll, factor, factorp):
        n = 2 * yy + ll
        out = dot(gt4[n, c], call[...]) * factor + dot(gtp[n], callp[...]) * factorp
        value = dot(xt4[n, c], dv[...]) * factor + dot(xtp[n], dvp[...]) * factorp
        ssum[ll, yy, :, 0:256] = out[:, :256].astype(BF16)
        ssum[ll, yy, :, 256:384] = value[:, :128].astype(BF16)
        ssum[ll, yy, :, 384:640] = out[:, 256:].astype(BF16)
        ssum[ll, yy, :, 640:768] = value[:, 128:].astype(BF16)

    def add(*pieces):
        total = pieces[0].astype(F32)
        for piece in pieces[1:]:
            total += piece.astype(F32)
        return total

    def yp(step):
        return lax.rem(y + step + 4, 4)

    def hcols(hh):
        return pl.ds(mo(hh * 384, 128), 384)

    def xhl(step):
        there = xpos(step)
        return lax.div(there, 2), lax.rem(there, 2)

    parts = (pl.ds(0, 80), pl.ds(80, 80))
    bparts = (pl.ds(0, 64), pl.ds(64, 64))
    highs = (pl.ds(160, 64), pl.ds(224, 64))

    def a_one(q):
        far = yp(2)
        ds = parts[q]
        send(ssum.at[0, far, ds], a1r.at[0, ds], rsem, 25 * q, ydev(1))
        send(ssum.at[1, far, ds], a1r.at[1, ds], rsem, 25 * q + 1, ydev(-1))

    def a_direct(q):
        ds = parts[q]
        send(ssum.at[1, yp(1), ds], a2r.at[0, 1, ds], rsem, 25 * q + 2, ydev(1))
        send(ssum.at[0, yp(-1), ds], a2r.at[1, 0, ds], rsem, 25 * q + 3, ydev(-1))

    def a_two(q):
        ds = parts[q]
        for way in range(2):
            step = 1 - 2 * way
            arrived(a1r.at[way, ds], rsem, 25 * q + way, ydev(step))
            a2s[way, ds, :] = add(ssum[way, yp(step), ds, :], a1r[way, ds, :]).astype(BF16)
            send(a2s.at[way, ds], a2r.at[way, way, ds], rsem, 25 * q + 4 + way, ydev(step))

    def a_three(q):
        ds = parts[q]
        arrived(a2r.at[0, 1, ds], rsem, 25 * q + 2, ydev(1))
        arrived(a2r.at[1, 0, ds], rsem, 25 * q + 3, ydev(-1))
        for way in range(2):
            arrived(a2r.at[way, way, ds], rsem, 25 * q + 4 + way, ydev(1 - 2 * way))
        for ll in range(2):
            ua[ll, ds, :] = add(ssum[ll, y, ds, :], a2r[0, ll, ds, :], a2r[1, ll, ds, :]).astype(BF16)
        for k in range(1, 4):
            ph, pll = xhl(k)
            send(ua.at[pll, ds, hcols(ph)], a4r.at[k - 1, ds], rsem, 25 * q + 5 + k, xdev(k))

    def a_four(q):
        ds = parts[q]
        for k in range(1, 4):
            arrived(a4r.at[k - 1, ds], rsem, 25 * q + 5 + k, xdev(k))
        total = add(ua[l, ds, hcols(h)], a4r[0, ds, :], a4r[1, ds, :], a4r[2, ds, :])
        outt_ref[ds, :] = total[:, :256]
        val_ref[ds, :] = total[:, 256:]

    pairs = (pl.ds(0, 2), pl.ds(2, 2))

    def s_high(q, pair, ll, hh):
        return ssum.at[ll, pairs[pair], highs[q], hcols(hh)]

    def b_one(q):
        ph, pll = xhl(2)
        for way in range(2):
            send(s_high(q, way, pll, ph), b1r.at[pairs[way], bparts[q]], rsem, 25 * q + 10 + way, xdev(1 - 2 * way))

    def b_direct(q):
        for way in range(2):
            ph, pll = xhl(1 - 2 * way)
            send(s_high(q, 1 - way, pll, ph), b2r.at[way, pairs[1 - way], bparts[q]], rsem, 25 * q + 14 + way, xdev(1 - 2 * way))

    def b_two(q):
        ds = bparts[q]
        for way in range(2):
            step = 1 - 2 * way
            ph, pll = xhl(step)
            arrived(b1r.at[pairs[way], ds], rsem, 25 * q + 10 + way, xdev(step))
            for yy in (2 * way, 2 * way + 1):
                b2s[yy, ds, :] = add(ssum[pll, yy, highs[q], hcols(ph)], b1r[yy, ds, :]).astype(BF16)
            send(b2s.at[pairs[way], ds], b2r.at[way, pairs[way], ds], rsem, 25 * q + 18 + way, xdev(step))

    def b_three(q):
        ds = bparts[q]
        for way in range(2):
            arrived(b2r.at[way, pairs[1 - way], ds], rsem, 25 * q + 14 + way, xdev(1 - 2 * way))
            arrived(b2r.at[way, pairs[way], ds], rsem, 25 * q + 18 + way, xdev(1 - 2 * way))
        for yy in range(4):
            ub[yy, ds, :] = add(ssum[l, yy, highs[q], hcols(h)], b2r[0, yy, ds, :], b2r[1, yy, ds, :]).astype(BF16)
        for k in range(1, 4):
            send(ub.at[yp(k), ds], b4r.at[k - 1, ds], rsem, 25 * q + 21 + k, ydev(k))

    def b_four(q):
        ds = bparts[q]
        for k in range(1, 4):
            arrived(b4r.at[k - 1, ds], rsem, 25 * q + 21 + k, ydev(k))
        total = add(ub[y, ds, :], b4r[0, ds, :], b4r[1, ds, :], b4r[2, ds, :])
        outt_ref[highs[q], :] = total[:, :256]
        val_ref[highs[q], :] = total[:, 256:]

    local[1].wait()
    local[2].wait()
    softmax(h)
    pl.semaphore_wait(barrier, len(peers))
    ag_send(G, OWN, 1)
    ex_send(1, gsend)
    local[0].wait()
    ag_send(X, OWN, 1)
    w_first(1)
    ag_next(G, OWN, 1)
    ex_send(0, x_ref.at[oh])
    ex_wait(1)
    ag_send(G, OTHER, 1)
    ag_next(G, OWN, 2)
    w_second(1)
    ag_next(G, OTHER, 1)
    w_first(0)
    ag_next(G, OWN, 3)
    ag_next(X, OWN, 1)
    w_third(1)
    ag_next(G, OTHER, 2)
    ex_wait(0)
    ag_send(X, OTHER, 1)
    ex_send(2, q_ref.at[oh])
    ex_send(3, k_ref.at[oh])
    ag_wait(G, OWN, 4)
    transpose_half(gall, gt, OWN)
    turned_send(G, OWN)
    w_fourth(1)
    w_second(0)
    ag_next(G, OTHER, 3)
    ag_next(X, OWN, 2)
    w_last(1)
    local[4].wait()
    grad_contexts(OWN)
    ag_next(X, OTHER, 1)
    w_third(0)
    ex_wait(2)
    ex_wait(3)
    softmax(oh)
    early = len(sent)
    ag_wait(G, OTHER, 4)
    transpose_half(gall, gt, OTHER)
    turned_send(G, OTHER)
    ag_next(X, OWN, 3)
    grad_contexts(OTHER)
    grad_values()
    w_fourth(0)
    send(dv, dvp, csem, 4, core)
    ag_next(X, OTHER, 2)
    w_last(0)
    local[3].wait()
    dx_partial(OTHER)
    ag_wait(X, OWN, 4)
    values(OWN)
    dx_partial(OWN)
    ag_next(X, OTHER, 3)
    z_step(OTHER, 1)
    z_step(OWN, 1)
    g_gram()
    x_gram()
    transpose_half(xall, xt, OWN)
    turned_send(X, OWN)
    for part in range(2):
        turned_wait(G, part)
    drain(early)
    ag_wait(X, OTHER, 4)
    gathers = len(sent)
    values(OTHER)
    contexts()
    norm_send()
    send(call, callp, csem, 5, core)
    z_step(OTHER, 2)
    transpose_half(xall, xt, OTHER)
    turned_send(X, OTHER)
    z_step(OWN, 2)
    arrived(dvp, csem, 4, core)
    arrived(callp, csem, 5, core)
    for part in range(2):
        turned_wait(X, part)
    z_step(OTHER, 3)
    drain(gathers)
    before = len(sent)
    factor, factorp = norm_wait()

    block(yp(2), l, factor, factorp)
    block(yp(2), 1 - l, factor, factorp)
    a_one(0)
    a_one(1)

    def near(yy, carry):
        block(lax.rem(yy + y + 3, 4), l, factor, factorp)
        return carry

    lax.fori_loop(0, 3, near, 0, unroll=True)
    b_one(0)
    b_one(1)

    def rest(yy, carry):
        block(lax.rem(yy + y + 3, 4), 1 - l, factor, factorp)
        return carry

    lax.fori_loop(0, 3, rest, 0, unroll=True)
    a_direct(0)
    b_direct(0)
    z_step(OWN, 3)
    a_two(0)
    a_direct(1)
    b_two(0)
    b_direct(1)
    z_step(OTHER, 4)
    a_two(1)
    b_two(1)
    drain(before)
    first = len(sent)
    a_three(0)
    b_three(0)
    z_step(OWN, 4)
    gis[...] = z_final(OTHER)
    ex_send(4, gis)
    a_three(1)
    b_three(1)
    gi_ref[h] = z_final(OWN)
    drain(first)
    a_four(0)
    b_four(0)
    a_four(1)
    b_four(1)
    ex_wait(4)
    gi_ref[oh] = gir[...]
    for copy in sent:
        copy.wait_send()


def finish(outt_ref, val_ref, gi_ref, out_ref, value_ref, grad_ref):
    out_ref[...] = outt_ref[...]
    value_ref[...] = val_ref[...]
    grad_ref[...] = gi_ref[...]


def per_device(layer_input, out_grad, loss_weight, queries, keys, value_weight, output_weight, lengths):
    any_spec = pl.BlockSpec(memory_space=pl.ANY)
    smem = pl.BlockSpec(memory_space=pltpu.SMEM)
    vmem = pl.BlockSpec(memory_space=pltpu.VMEM)

    def buf(*shape, dtype=BF16):
        return pltpu.VMEM(shape, dtype)

    dma = pltpu.SemaphoreType.DMA
    out_t, value, grad_input = pl.pallas_call(
        kernel,
        out_shape=(
            jax.ShapeDtypeStruct((288, 256), F32),
            jax.ShapeDtypeStruct((288, 128), F32),
            jax.ShapeDtypeStruct((2, TOK, D), BF16),
        ),
        in_specs=[smem, smem, any_spec, vmem, any_spec, any_spec, any_spec, any_spec],
        out_specs=(vmem, vmem, vmem),
        scratch_shapes=[
            buf(SEQ, D), buf(SEQ, D), buf(8, 2, 288, SEQ), buf(8, 2, 288, SEQ), buf(8, 288, SEQ), buf(8, 288, SEQ),
            buf(TOK, D), buf(SEQ, 512), buf(SEQ, 256), buf(D, 256), buf(512, D),
            buf(4, SEQ, SEQ), buf(SEQ, 256), buf(SEQ, 512), buf(SEQ, 512), buf(512, SEQ), buf(256, SEQ),
            buf(SEQ, 256), buf(SEQ, 256),
            buf(SEQ, SEQ, dtype=F32), buf(128, 128, dtype=F32), buf(2, NZ, 1, 128, dtype=F32),
            buf(SEQ, D, dtype=F32), buf(16, TOK, D), buf(16, TOK, D), buf(TOK, D), buf(TOK, D), buf(2, 4, 288, 768),
            buf(2, 160, 768), buf(2, 160, 768), buf(2, 2, 160, 768), buf(2, 160, 768), buf(3, 160, 384),
            buf(4, 128, 384), buf(4, 128, 384), buf(2, 4, 128, 384), buf(4, 128, 384), buf(3, 128, 384),
            dma((5,)), dma((2, 5)), dma((2, 32)), dma((2, 18)), dma((2, 15)), dma((2, 16)), dma((2, 6)),
            dma((2, 50)),
        ],
        compiler_params=pltpu.CompilerParams(
            collective_id=0, has_side_effects=True, vmem_limit_bytes=60 * 1024 * 1024
        ),
        cost_estimate=pl.CostEstimate(flops=5_000_000_000, bytes_accessed=12_000_000, transcendentals=1_000_000),
        name="clipped_grads",
    )(loss_weight, lengths, layer_input, out_grad, queries, keys, value_weight, output_weight)
    out_t, value, grad_input = pl.pallas_call(
        finish,
        out_shape=(
            jax.ShapeDtypeStruct((288, 256), F32),
            jax.ShapeDtypeStruct((288, 128), F32),
            jax.ShapeDtypeStruct((2, TOK, D), BF16),
        ),
        in_specs=[vmem] * 3,
        out_specs=(vmem,) * 3,
        compiler_params=pltpu.CompilerParams(vmem_limit_bytes=60 * 1024 * 1024),
        name="finish",
    )(out_t, value, grad_input)
    return out_t.T, value, grad_input


def solution(mesh):
    in_specs = (
        P("dp", "tensor", None),
        P("dp", "tensor", None),
        P("dp"),
        P("dp", None, "tensor"),
        P("dp", None, "tensor"),
        P(None, "tensor"),
        P("tensor", None),
        P("dp"),
    )
    out_specs = (P("tensor", "dp"), P("dp", "tensor"), P("dp", "tensor", None))
    return jax.shard_map(
        per_device, mesh=mesh, in_specs=in_specs, out_specs=out_specs, check_vma=False
    )
```
